256 devices in a mesh: batch: 32 (over z, y_hi, core), feat: 8 (over y_lo, x).
Axes of the slice: x: 4, y: 4 (y_hi: 2, y_lo: 2; y = y_hi * 2 + y_lo), z: 8, core: 2. Of those that a mesh axis runs over, the one named last changes fastest.
Arguments:
- view_a: bfloat16 [4096, 8192], P('batch', 'feat'), may hold values from -256 to 256
- view_b: bfloat16 [4096, 8192], P('batch', 'feat'), may hold values from -256 to 256
Outputs:
- grad_a: bfloat16 [4096, 8192], P('batch', 'feat')
- grad_b: bfloat16 [4096, 8192], P('batch', 'feat')
- loss: float32 [], replicated
The draws below stay inside these ranges and needn't reach their ends.
All inputs are finite; a program needn't handle non-finite values.
Results may differ from the reference program's by a relative error of at most 0.006.
Values may be sent and summed in bfloat16 or wider, within the bound.
No kernel may reach another device: no remote copies, remote signals or barrier semaphores. Data moves between devices by JAX's collectives and lax.ppermute only.
A program may use at most 128 MiB of HBM per device.

```python
import math
import jax
import jax.numpy as jnp
from jax import lax

WIDTH = 8192
MOLECULES = 4096


factor_count = 8


def shared_parts(key, row_high, ramp, factor_amp):
    keys = jax.random.split(key, 8)
    normal_part = jax.random.normal(keys[0], (MOLECULES, WIDTH), jnp.float32)
    base = normal_part
    feature_place = jnp.arange(WIDTH, dtype=jnp.float32) / WIDTH
    factor_rows = jax.random.normal(keys[5], (MOLECULES, factor_count), jnp.float32)
    loadings = jax.random.normal(keys[6], (factor_count, WIDTH), jnp.float32)
    centers = jax.random.uniform(keys[7], (factor_count, 1), jnp.float32, 0.0, 1.0)
    profile = 0.4 + 2.0 * jnp.exp(-(feature_place[None, :] - centers) ** 2 / 0.02)
    loadings = factor_amp * profile * loadings
    for index in range(factor_count):
        base = base + factor_rows[:, index:index + 1] * loadings[index:index + 1, :]
    position = jnp.arange(MOLECULES, dtype=jnp.float32) / MOLECULES
    row_scale = jnp.exp(jax.random.uniform(keys[2], (MOLECULES,), jnp.float32, 0.0, math.log(row_high))) * (1.0 + ramp * position)
    offset = jax.random.uniform(keys[3], (1, WIDTH), jnp.float32, -2.0, 2.0)
    noise_level = jnp.exp(jax.random.uniform(keys[4], (WIDTH,), jnp.float32, math.log(0.05), math.log(0.2))) * (1.0 + 2.5 * feature_place)
    return (base, row_scale[:, None], offset, noise_level[None, :])


def draw_view_a(key, part):
    base, row_scale, offset, noise_level = shared_parts(key, 10.0, 2.0, 0.08)
    key = jax.random.fold_in(key, 11)
    noise = jax.random.normal(key, (MOLECULES, WIDTH), jnp.float32)
    values = row_scale * (base + noise_level * noise) + offset
    return jnp.clip(values, -250.0, 250.0).astype(jnp.bfloat16)


def draw_view_b(key, part):
    base, row_scale, offset, noise_level = shared_parts(key, 10.0, 2.0, 0.08)
    key = jax.random.fold_in(key, 23)
    noise = jax.random.normal(key, (MOLECULES, WIDTH), jnp.float32)
    values = row_scale * (base + noise_level * noise) + offset
    return jnp.clip(values, -250.0, 250.0).astype(jnp.bfloat16)


def setup_inputs(seed: int = 0) -> dict:
    arg_keys = jax.random.split(jax.random.key(seed), 3)
    return {
        "view_a": draw_view_a(jax.random.fold_in(arg_keys[2], 71), 0),
        "view_b": draw_view_b(jax.random.fold_in(arg_keys[2], 71), 0),
    }


redund_weight = 0.0051
eps_var = 1e-05

def standardize(values, count):
    floats = values.astype(jnp.float32)
    mean_value = lax.optimization_barrier(jnp.sum(floats, 0)) / count
    var_value = lax.optimization_barrier(jnp.sum(floats * floats, 0)) / count - mean_value * mean_value
    rstd = lax.rsqrt(var_value + eps_var)
    return (((floats - mean_value) * rstd).astype(jnp.bfloat16), rstd)

def backward(grad_norm, normed, rstd, count, scale):
    normed_f = normed.astype(jnp.float32)
    mean_grad = lax.optimization_barrier(jnp.sum(grad_norm, 0)) / count
    mean_cross = lax.optimization_barrier(jnp.sum(grad_norm * normed_f, 0)) / count
    return (scale * rstd * (grad_norm - mean_grad - normed_f * mean_cross)).astype(jnp.bfloat16)

def reference(view_a, view_b):
    count = view_a.shape[0]
    norm_a, rstd_a = standardize(view_a, count)
    norm_b, rstd_b = standardize(view_b, count)
    corr_diag = lax.optimization_barrier(jnp.sum(norm_a.astype(jnp.float32) * norm_b.astype(jnp.float32), 0)) / count
    gram_a = jnp.dot(norm_a, norm_a.T, preferred_element_type=jnp.float32)
    gram_b = jnp.dot(norm_b, norm_b.T, preferred_element_type=jnp.float32)
    diag_loss = jnp.sum((1.0 - corr_diag) ** 2) - redund_weight * jnp.sum(corr_diag * corr_diag)
    frobenius = jnp.sum(gram_a * gram_b)
    loss = diag_loss + redund_weight * frobenius / (count * count)
    low_a = gram_a.astype(jnp.bfloat16)
    low_b = gram_b.astype(jnp.bfloat16)
    diag_grad = -2.0 * (1.0 - corr_diag) - 2.0 * redund_weight * corr_diag
    coupling = 2.0 * redund_weight / (count * count)
    grad_norm_a = diag_grad * norm_b.astype(jnp.float32) / count + coupling * jnp.dot(low_b, norm_a, preferred_element_type=jnp.float32)
    grad_norm_b = diag_grad * norm_a.astype(jnp.float32) / count + coupling * jnp.dot(low_a, norm_b, preferred_element_type=jnp.float32)
    scale = count * count / (redund_weight * WIDTH)
    grad_a = backward(grad_norm_a, norm_a, rstd_a, count, scale)
    grad_b = backward(grad_norm_b, norm_b, rstd_b, count, scale)
    return (grad_a, grad_b, loss)
```

```python
import jax
import jax.numpy as jnp
from jax import lax
from jax.sharding import Mesh, PartitionSpec as P

WIDTH = 8192

redund_weight = 0.0051
eps_var = 1e-05

ROWS = ("z", "yh", "c")
FEAT = ("yl", "x")
SWAP = [(0, 1), (1, 0)]


def batch_sum(values):
    values = values + lax.ppermute(values, "c", SWAP)
    chips = lax.axis_size("z") * lax.axis_size("yh")
    parts = lax.all_to_all(
        jnp.broadcast_to(values[None], (chips,) + values.shape), ("z", "yh"), 0, 0
    )
    return jnp.sum(parts, 0)


def shards(view_a, view_b):
    row_count, width = view_a.shape
    batch_total = row_count * lax.axis_size(ROWS)
    feats = lax.axis_size(FEAT)
    both = jnp.stack([view_a, view_b])
    gathered = lax.all_gather(both, ("z", "c"))
    other = lax.ppermute(both, "yh", SWAP)

    floats = both.astype(jnp.float32)
    moments = batch_sum(jnp.stack([jnp.sum(floats, 1), jnp.sum(floats * floats, 1)]))
    mean = moments[0] / batch_total
    rstd = lax.rsqrt(moments[1] / batch_total - mean * mean + eps_var)

    def standardize(values, view):
        return ((values.astype(jnp.float32) - mean[view]) * rstd[view]).astype(jnp.bfloat16)

    own = [standardize(both[v], v) for v in range(2)]
    cross_sum = batch_sum(
        jnp.sum(own[0].astype(jnp.float32) * own[1].astype(jnp.float32), 0)[None]
    )[0]
    corr_diag = cross_sum / batch_total
    diag_part = jnp.sum((1.0 - corr_diag) ** 2) - redund_weight * jnp.sum(corr_diag * corr_diag)
    diag_grad = -2.0 * (1.0 - corr_diag) - 2.0 * redund_weight * corr_diag

    rows = [jnp.concatenate([own[v], standardize(other[v], v)]) for v in range(2)]
    cols = [standardize(gathered[:, v], v).reshape(-1, width) for v in range(2)]
    panel = cols[0].shape[0]
    piece = 2 * row_count // feats
    grams = [
        lax.dot_general(
            rows[v], cols[v], (((1,), (1,)), ((), ())), preferred_element_type=jnp.float32
        )
        .astype(jnp.bfloat16)
        .reshape(feats, piece, panel)
        for v in range(2)
    ]
    pieces = lax.all_to_all(jnp.stack(grams, 1), FEAT, 0, 0)
    summed = jnp.sum(pieces.astype(jnp.float32), 0)
    frob = jnp.sum(summed[0] * summed[1])
    loss_part = (
        diag_part / lax.axis_size(ROWS) + redund_weight * frob / (batch_total * batch_total)
    )
    high = lax.reduce_precision(loss_part, 8, 7)
    middle = lax.reduce_precision(loss_part - high, 8, 7)
    low = lax.reduce_precision(loss_part - high - middle, 8, 7)
    lane = lax.broadcasted_iota(jnp.int32, (2, piece, 128), 2)
    extra = jnp.where(lane == 0, high, jnp.where(lane == 1, middle, jnp.where(lane == 2, low, 0.0)))
    sent = jnp.concatenate([summed, extra], 2).astype(jnp.bfloat16)
    full = lax.all_to_all(jnp.broadcast_to(sent[None], (feats,) + sent.shape), FEAT, 0, 0)
    low_gram = [full[:, v, :, :panel].reshape(2 * row_count, panel) for v in range(2)]
    loss_row = jnp.sum(full[:, 0, 0, panel : panel + 3].astype(jnp.float32))

    coupling = 2.0 * redund_weight / (batch_total * batch_total)
    products = [
        coupling * jnp.dot(low_gram[1 - v], cols[v], preferred_element_type=jnp.float32)
        for v in range(2)
    ]
    received = lax.ppermute(
        jnp.stack([p[row_count:] for p in products]).astype(jnp.bfloat16), "yh", SWAP
    )
    sums = []
    mine = []
    for v in range(2):
        product = products[v]
        mine.append(
            product[:row_count] + diag_grad * own[1 - v].astype(jnp.float32) / batch_total
        )
        theirs = product[row_count:]
        sums.append(jnp.sum(mine[v], 0) + jnp.sum(theirs, 0))
        sums.append(
            jnp.sum(mine[v] * own[v].astype(jnp.float32), 0)
            + jnp.sum(theirs * rows[v][row_count:].astype(jnp.float32), 0)
        )
    sums.append(jnp.full((width,), loss_row))
    back = batch_sum(jnp.stack(sums))
    scale = batch_total * batch_total / (redund_weight * WIDTH)
    grads = [
        (
            scale
            * rstd[v]
            * (
                mine[v]
                + received[v].astype(jnp.float32)
                - back[2 * v] / batch_total
                - own[v].astype(jnp.float32) * (back[2 * v + 1] / batch_total)
            )
        ).astype(jnp.bfloat16)
        for v in range(2)
    ]
    return grads[0], grads[1], back[4, 0]


def solution(mesh):
    fine = Mesh(mesh.devices.reshape(8, 2, 2, 2, 4), ROWS + FEAT)
    return jax.shard_map(
        shards,
        mesh=fine,
        in_specs=(P(ROWS, FEAT), P(ROWS, FEAT)),
        out_specs=(P(ROWS, FEAT), P(ROWS, FEAT), P()),
        check_vma=False,
    )
```

```python
import jax
import jax.numpy as jnp
from jax import lax
from jax.experimental import pallas as pl
from jax.experimental.pallas import tpu as pltpu
from jax.sharding import Mesh, PartitionSpec as P

WIDTH = 8192

redund_weight = 0.0051
eps_var = 1e-05

ROWS = ("z", "yh", "c")
FEAT = ("yl", "x")
SWAP = [(0, 1), (1, 0)]
LIMIT = 48 * 1024 * 1024


def pair_sum(values):
    values = values + lax.ppermute(values, "c", SWAP)
    return values + lax.ppermute(values, "yh", SWAP)


def spread(values):
    count = lax.axis_size("z")
    return lax.all_to_all(jnp.broadcast_to(values[None], (count,) + values.shape), "z", 0, 0)


def batch_sum(values):
    return jnp.sum(spread(pair_sum(values)), 0)


def standardize(values, mean, rstd):
    return ((values.astype(jnp.float32) - mean) * rstd).astype(jnp.bfloat16)


def gram_kernel(mean, rstd, raw, own, other, cols, rows, parts):
    count = own.shape[1]

    @pl.when(pl.program_id(0) == 0)
    def _():
        for v in range(2):
            rows[v, :count] = standardize(own[v], mean[v : v + 1], rstd[v : v + 1])
            rows[v, count:] = standardize(other[v], mean[v : v + 1], rstd[v : v + 1])

    for v in range(2):
        for k in range(raw.shape[0]):
            cols[v, k * count : (k + 1) * count] = standardize(
                raw[k, v], mean[v : v + 1], rstd[v : v + 1]
            )
        gram = lax.dot_general(
            rows[v], cols[v], (((1,), (1,)), ((), ())), preferred_element_type=jnp.float32
        )
        feats, _, piece, width = parts.shape
        parts[:, v] = gram.astype(jnp.bfloat16).reshape(feats, piece, width)


def gram_parts(mean, rstd, gathered, own, other, feats):
    blocks, _, count, width = gathered.shape
    step = 2
    piece = 2 * count // feats
    whole = lambda shape: pl.BlockSpec(shape, lambda k: (0,) * len(shape))
    return pl.pallas_call(
        gram_kernel,
        grid=(blocks // step,),
        in_specs=[
            whole((2, width)),
            whole((2, width)),
            pl.BlockSpec((step, 2, count, width), lambda k: (k, 0, 0, 0)),
            whole((2, count, width)),
            whole((2, count, width)),
        ],
        out_specs=[
            pl.BlockSpec((2, step * count, width), lambda k: (0, k, 0)),
            whole((2, 2 * count, width)),
            pl.BlockSpec((feats, 2, piece, step * count), lambda k: (0, 0, 0, k)),
        ],
        out_shape=[
            jax.ShapeDtypeStruct((2, blocks * count, width), jnp.bfloat16),
            jax.ShapeDtypeStruct((2, 2 * count, width), jnp.bfloat16),
            jax.ShapeDtypeStruct((feats, 2, piece, blocks * count), jnp.bfloat16),
        ],
        compiler_params=pltpu.CompilerParams(vmem_limit_bytes=LIMIT),
        name="gram",
    )(mean, rstd, gathered, own, other)


def reduce_kernel(weight, diag, pieces, sent):
    feats, _, piece, panel = pieces.shape
    total = []
    for v in range(2):
        total.append(pieces[0, v].astype(jnp.float32))
        for w in range(1, feats):
            total[v] = total[v] + pieces[w, v].astype(jnp.float32)
    frob = jnp.sum(total[0] * total[1], keepdims=True)
    loss_part = diag[...] + weight * frob
    part = jnp.broadcast_to(loss_part, (piece, 128))
    high = part.astype(jnp.bfloat16).astype(jnp.float32)
    middle = (part - high).astype(jnp.bfloat16).astype(jnp.float32)
    low = part - high - middle
    lane = lax.broadcasted_iota(jnp.int32, part.shape, 1)
    extra = jnp.where(lane == 0, high, jnp.where(lane == 1, middle, jnp.where(lane == 2, low, 0.0)))
    extra = extra.astype(jnp.bfloat16)
    for v in range(2):
        low_gram = total[v].astype(jnp.bfloat16)
        for w in range(feats):
            sent[w, v, :, :panel] = low_gram
            sent[w, v, :, panel:] = extra


def reduce_parts(pieces, diag, weight):
    feats, _, piece, panel = pieces.shape
    return pl.pallas_call(
        lambda *refs: reduce_kernel(weight, *refs),
        out_shape=jax.ShapeDtypeStruct((feats, 2, piece, panel + 128), jnp.bfloat16),
        compiler_params=pltpu.CompilerParams(vmem_limit_bytes=LIMIT),
        name="reduce",
    )(diag, pieces)


def product_kernel(coupling, total_rows, full, tail, cols, rows, diag_grad, mine, sent, sums, acc):
    step = pl.program_id(0)
    feats, _, piece, depth = full.shape
    count = rows.shape[1] // 2
    for v in range(2):
        low_gram = full[:, 1 - v].reshape(feats * piece, depth)
        product = jnp.dot(low_gram, cols[v], preferred_element_type=jnp.float32)

        @pl.when(step == 0)
        def _():
            acc[v] = product

        @pl.when(step > 0)
        def _():
            acc[v] += product

    @pl.when(step == pl.num_programs(0) - 1)
    def _():
        for v in range(2):
            near = coupling * acc[v, :count] + diag_grad[...] * (
                rows[1 - v, :count].astype(jnp.float32) * (1.0 / total_rows)
            )
            far = coupling * acc[v, count:]
            mine[v] = near
            sent[v] = far.astype(jnp.bfloat16)
            sums[2 * v : 2 * v + 1] = jnp.sum(near, 0, keepdims=True) + jnp.sum(
                far, 0, keepdims=True
            )
            sums[2 * v + 1 : 2 * v + 2] = jnp.sum(
                near * rows[v, :count].astype(jnp.float32), 0, keepdims=True
            ) + jnp.sum(far * rows[v, count:].astype(jnp.float32), 0, keepdims=True)
        first = tail[:, 0, 0:1, :].astype(jnp.float32).reshape(feats, 128)
        loss = jnp.sum(first, keepdims=True)
        sums[4:8] = jnp.broadcast_to(loss, (4, sums.shape[1]))


def products(full, cols, rows, diag_grad, coupling, total_rows):
    feats, _, piece, wide = full.shape
    _, panel, width = cols.shape
    count = rows.shape[1] // 2
    depth = 256
    whole = lambda shape: pl.BlockSpec(shape, lambda k: (0,) * len(shape))
    return pl.pallas_call(
        lambda *refs: product_kernel(coupling, total_rows, *refs),
        grid=(panel // depth,),
        in_specs=[
            pl.BlockSpec((feats, 2, piece, depth), lambda k: (0, 0, 0, k)),
            pl.BlockSpec((feats, 2, piece, 128), lambda k: (0, 0, 0, panel // 128)),
            pl.BlockSpec((2, depth, width), lambda k: (0, k, 0)),
            whole((2, 2 * count, width)),
            whole((1, width)),
        ],
        out_specs=[
            whole((2, count, width)),
            whole((2, count, width)),
            whole((8, width)),
        ],
        out_shape=[
            jax.ShapeDtypeStruct((2, count, width), jnp.float32),
            jax.ShapeDtypeStruct((2, count, width), jnp.bfloat16),
            jax.ShapeDtypeStruct((8, width), jnp.float32),
        ],
        scratch_shapes=[pltpu.VMEM((2, 2 * count, width), jnp.float32)],
        compiler_params=pltpu.CompilerParams(vmem_limit_bytes=LIMIT),
        name="products",
    )(full, full, cols, rows, diag_grad)


def final_kernel(scale, total_rows, parts, rstd, mine, received, rows, grad_a, grad_b, loss):
    total = parts[0]
    for k in range(1, parts.shape[0]):
        total = total + parts[k]
    total = total * (1.0 / total_rows)
    count = mine.shape[1]
    for v, out in ((0, grad_a), (1, grad_b)):
        out[...] = (
            (scale * rstd[v : v + 1])
            * (
                mine[v]
                + received[v].astype(jnp.float32)
                - total[2 * v : 2 * v + 1]
                - rows[v, :count].astype(jnp.float32) * total[2 * v + 1 : 2 * v + 2]
            )
        ).astype(jnp.bfloat16)
    loss[...] = total[4:5, :128] * total_rows


def finish(parts, rstd, mine, received, rows, scale, total_rows):
    _, count, width = mine.shape
    return pl.pallas_call(
        lambda *refs: final_kernel(scale, total_rows, *refs),
        out_shape=[
            jax.ShapeDtypeStruct((count, width), jnp.bfloat16),
            jax.ShapeDtypeStruct((count, width), jnp.bfloat16),
            jax.ShapeDtypeStruct((1, 128), jnp.float32),
        ],
        compiler_params=pltpu.CompilerParams(vmem_limit_bytes=LIMIT),
        name="finish",
    )(parts, rstd, mine, received, rows)


def shards(view_a, view_b):
    row_count, _ = view_a.shape
    batch_total = row_count * lax.axis_size(ROWS)
    feats = lax.axis_size(FEAT)
    both = jnp.stack([view_a, view_b])
    gathered = lax.all_gather(both, ("z", "c"))
    other = lax.ppermute(both, "yh", SWAP)

    floats = both.astype(jnp.float32)
    moments = batch_sum(jnp.stack([jnp.sum(floats, 1), jnp.sum(floats * floats, 1)]))
    mean = moments[0] / batch_total
    rstd = lax.rsqrt(moments[1] / batch_total - mean * mean + eps_var)

    own_a = standardize(view_a, mean[0], rstd[0]).astype(jnp.float32)
    own_b = standardize(view_b, mean[1], rstd[1]).astype(jnp.float32)
    corr_diag = batch_sum(jnp.sum(own_a * own_b, 0)[None]) / batch_total
    diag_part = jnp.sum((1.0 - corr_diag) ** 2) - redund_weight * jnp.sum(corr_diag * corr_diag)
    diag_grad = -2.0 * (1.0 - corr_diag) - 2.0 * redund_weight * corr_diag
    diag_share = (diag_part / lax.axis_size(ROWS)).reshape(1, 1)

    cols, rows, parts = gram_parts(mean, rstd, gathered, both, other, feats)
    pieces = lax.all_to_all(parts, FEAT, 0, 0)
    sent = reduce_parts(pieces, diag_share, redund_weight / (batch_total * batch_total))
    full = lax.all_to_all(sent, FEAT, 0, 0)
    coupling = 2.0 * redund_weight / (batch_total * batch_total)
    mine, leaving, sums = products(full, cols, rows, diag_grad, coupling, batch_total)
    received = lax.ppermute(leaving, "yh", SWAP)
    back = spread(pair_sum(sums))
    scale = batch_total * batch_total / (redund_weight * WIDTH)
    grad_a, grad_b, loss = finish(back, rstd, mine, received, rows, scale, batch_total)
    return grad_a, grad_b, loss[0, 0]


def solution(mesh):
    fine = Mesh(mesh.devices.reshape(8, 2, 2, 2, 4), ROWS + FEAT)
    return jax.shard_map(
        shards,
        mesh=fine,
        in_specs=(P(ROWS, FEAT), P(ROWS, FEAT)),
        out_specs=(P(ROWS, FEAT), P(ROWS, FEAT), P()),
        check_vma=False,
    )
```

```python
import jax
import jax.numpy as jnp
from jax import lax
from jax.experimental import pallas as pl
from jax.experimental.pallas import tpu as pltpu
from jax.sharding import Mesh, PartitionSpec as P

WIDTH = 8192

redund_weight = 0.0051
eps_var = 1e-05

ROWS = ("z", "yh", "c")
FEAT = ("yl", "x")
SWAP = [(0, 1), (1, 0)]
LIMIT = 40 * 1024 * 1024
VMEM = pl.BlockSpec(memory_space=pltpu.VMEM)
ANY = pl.BlockSpec(memory_space=pl.ANY)


def pair_sum(values):
    values = values + lax.ppermute(values, "c", SWAP)
    return values + lax.ppermute(values, "yh", SWAP)


def spread(values):
    count = lax.axis_size("z")
    return lax.all_to_all(jnp.broadcast_to(values[None], (count,) + values.shape), "z", 0, 0)


def batch_sum(values):
    return jnp.sum(spread(pair_sum(values)), 0)


def standardize(values, mean, rstd):
    return ((values.astype(jnp.float32) - mean) * rstd).astype(jnp.bfloat16)


def start_kernel(view_a, view_b, both, moments):
    for v, view in enumerate((view_a, view_b)):
        values = view[...]
        both[v] = values
        floats = values.astype(jnp.float32)
        moments[v : v + 1] = jnp.sum(floats, 0, keepdims=True)
        moments[v + 2 : v + 3] = jnp.sum(floats * floats, 0, keepdims=True)


def start(view_a, view_b):
    return pl.pallas_call(
        start_kernel,
        in_specs=[VMEM] * 2,
        out_specs=[VMEM] * 2,
        out_shape=[
            jax.ShapeDtypeStruct((2,) + view_a.shape, view_a.dtype),
            jax.ShapeDtypeStruct((4, view_a.shape[1]), jnp.float32),
        ],
        compiler_params=pltpu.CompilerParams(vmem_limit_bytes=LIMIT),
        name="start",
    )(view_a, view_b)


def gram_kernel(step, mean, rstd, own, other, source, cols, rows, parts, raw, sems):
    blocks, _, count, _ = raw.shape
    piece = parts.shape[2]
    copies = [
        pltpu.make_async_copy(source.at[pl.ds(k, step)], raw.at[pl.ds(k, step)], sems.at[k // step])
        for k in range(0, blocks, step)
    ]
    for copy in copies:
        copy.start()
    for v in range(2):
        rows[v, :count] = standardize(own[v], mean[v : v + 1], rstd[v : v + 1])
        rows[v, count:] = standardize(other[v], mean[v : v + 1], rstd[v : v + 1])
    for n, copy in enumerate(copies):
        copy.wait()
        first, last = n * step * count, (n + 1) * step * count
        for v in range(2):
            for k in range(n * step, (n + 1) * step):
                cols[v, k * count : (k + 1) * count] = standardize(
                    raw[k, v], mean[v : v + 1], rstd[v : v + 1]
                )
            gram = lax.dot_general(
                cols[v, first:last],
                rows[v],
                (((1,), (1,)), ((), ())),
                preferred_element_type=jnp.float32,
            )
            parts[first // piece : last // piece, v] = gram.astype(jnp.bfloat16).reshape(
                (last - first) // piece, piece, 2 * count
            )


def gram_parts(mean, rstd, gathered, own, other, feats):
    blocks, _, count, width = gathered.shape
    step = 4
    return pl.pallas_call(
        lambda *refs: gram_kernel(step, *refs),
        in_specs=[VMEM] * 4 + [ANY],
        out_specs=[VMEM] * 3,
        out_shape=[
            jax.ShapeDtypeStruct((2, blocks * count, width), jnp.bfloat16),
            jax.ShapeDtypeStruct((2, 2 * count, width), jnp.bfloat16),
            jax.ShapeDtypeStruct((feats, 2, blocks * count // feats, 2 * count), jnp.bfloat16),
        ],
        scratch_shapes=[
            pltpu.VMEM(gathered.shape, jnp.bfloat16),
            pltpu.SemaphoreType.DMA((blocks // step,)),
        ],
        compiler_params=pltpu.CompilerParams(vmem_limit_bytes=LIMIT),
        name="gram",
    )(mean, rstd, own, other, gathered)


def reduce_kernel(weight, diag, pieces, sent):
    feats, _, piece, row_count = pieces.shape
    total = []
    for v in range(2):
        total.append(pieces[0, v].astype(jnp.float32))
        for w in range(1, feats):
            total[v] = total[v] + pieces[w, v].astype(jnp.float32)
    frob = jnp.sum(total[0] * total[1], keepdims=True)
    part = jnp.broadcast_to(diag[...] + weight * frob, (16, piece))
    high = part.astype(jnp.bfloat16).astype(jnp.float32)
    middle = (part - high).astype(jnp.bfloat16).astype(jnp.float32)
    low = part - high - middle
    lane = lax.broadcasted_iota(jnp.int32, part.shape, 1)
    extra = jnp.where(lane == 0, high, jnp.where(lane == 1, middle, jnp.where(lane == 2, low, 0.0)))
    extra = extra.astype(jnp.bfloat16)
    for v in range(2):
        low_gram = total[v].T.astype(jnp.bfloat16)
        for w in range(feats):
            sent[w, v, :row_count] = low_gram
            sent[w, v, row_count:] = extra


def reduce_parts(pieces, diag, weight):
    feats, _, piece, row_count = pieces.shape
    return pl.pallas_call(
        lambda *refs: reduce_kernel(weight, *refs),
        in_specs=[VMEM] * 2,
        out_specs=VMEM,
        out_shape=jax.ShapeDtypeStruct((feats, 2, row_count + 16, piece), jnp.bfloat16),
        compiler_params=pltpu.CompilerParams(vmem_limit_bytes=LIMIT),
        name="reduce",
    )(diag, pieces)


def product_kernel(coupling, total_rows, full, cols, rows, diag_grad, mine, sent, sums):
    feats, _, _, piece = full.shape
    count = rows.shape[1] // 2
    width = cols.shape[2]
    chunk = 512
    for v in range(2):
        for f in range(0, width, chunk):
            here = slice(f, f + chunk)
            product = None
            for w in range(feats):
                term = jnp.dot(
                    full[w, 1 - v, : 2 * count],
                    cols[v, w * piece : (w + 1) * piece, here],
                    preferred_element_type=jnp.float32,
                )
                product = term if product is None else product + term
            product = coupling * product
            near = product[:count] + diag_grad[:, here] * (
                rows[1 - v, :count, here].astype(jnp.float32) * (1.0 / total_rows)
            )
            far = product[count:]
            mine[v, :, here] = near
            sent[v, :, here] = far.astype(jnp.bfloat16)
            plain = jnp.sum(near, 0, keepdims=True) + jnp.sum(far, 0, keepdims=True)
            cross = jnp.sum(
                near * rows[v, :count, here].astype(jnp.float32), 0, keepdims=True
            ) + jnp.sum(far * rows[v, count:, here].astype(jnp.float32), 0, keepdims=True)
            for k in range(chunk // 128):
                row = 2 * v * (width // 128) + f // 128 + k
                sums[row : row + 1] = plain[:, k * 128 : (k + 1) * 128]
                row += width // 128
                sums[row : row + 1] = cross[:, k * 128 : (k + 1) * 128]
    pieces = full[:, 0, 2 * count : 2 * count + 16, :128].astype(jnp.float32)
    loss = jnp.sum(pieces[:, 0:1, :].reshape(feats, 128), keepdims=True)
    last = 4 * (width // 128)
    sums[last : last + 8] = jnp.broadcast_to(loss, (8, 128))


def products(full, cols, rows, diag_grad, coupling, total_rows):
    _, _, width = cols.shape
    count = rows.shape[1] // 2
    return pl.pallas_call(
        lambda *refs: product_kernel(coupling, total_rows, *refs),
        in_specs=[VMEM] * 4,
        out_specs=[VMEM] * 3,
        out_shape=[
            jax.ShapeDtypeStruct((2, count, width), jnp.float32),
            jax.ShapeDtypeStruct((2, count, width), jnp.bfloat16),
            jax.ShapeDtypeStruct((4 * (width // 128) + 8, 128), jnp.float32),
        ],
        compiler_params=pltpu.CompilerParams(vmem_limit_bytes=LIMIT),
        name="products",
    )(full, cols, rows, diag_grad)


def final_kernel(scale, total_rows, parts, rstd, mine, received, rows, grad_a, grad_b, loss):
    total = parts[0]
    for k in range(1, parts.shape[0]):
        total = total + parts[k]
    total = total * (1.0 / total_rows)
    _, count, width = mine.shape
    lanes = width // 128
    for v, out in ((0, grad_a), (1, grad_b)):
        for k in range(lanes):
            here = slice(k * 128, (k + 1) * 128)
            plain = 2 * v * lanes + k
            cross = plain + lanes
            out[:, here] = (
                (scale * rstd[v : v + 1, here])
                * (
                    mine[v, :, here]
                    + received[v, :, here].astype(jnp.float32)
                    - total[plain : plain + 1]
                    - rows[v, :count, here].astype(jnp.float32) * total[cross : cross + 1]
                )
            ).astype(jnp.bfloat16)
    loss[...] = total[4 * lanes : 4 * lanes + 1] * total_rows


def finish(parts, rstd, mine, received, rows, scale, total_rows):
    _, count, width = mine.shape
    return pl.pallas_call(
        lambda *refs: final_kernel(scale, total_rows, *refs),
        in_specs=[VMEM] * 5,
        out_specs=[VMEM] * 3,
        out_shape=[
            jax.ShapeDtypeStruct((count, width), jnp.bfloat16),
            jax.ShapeDtypeStruct((count, width), jnp.bfloat16),
            jax.ShapeDtypeStruct((1, 128), jnp.float32),
        ],
        compiler_params=pltpu.CompilerParams(vmem_limit_bytes=LIMIT),
        name="finish",
    )(parts, rstd, mine, received, rows)


def shards(view_a, view_b):
    row_count, _ = view_a.shape
    batch_total = row_count * lax.axis_size(ROWS)
    feats = lax.axis_size(FEAT)
    both, moments = start(view_a, view_b)
    gathered = lax.all_gather(both, ("z", "c"))
    other = lax.ppermute(both, "yh", SWAP)

    moments = batch_sum(moments)
    mean = moments[:2] / batch_total
    rstd = lax.rsqrt(moments[2:] / batch_total - mean * mean + eps_var)

    own_a = standardize(view_a, mean[0], rstd[0]).astype(jnp.float32)
    own_b = standardize(view_b, mean[1], rstd[1]).astype(jnp.float32)
    corr_diag = batch_sum(jnp.sum(own_a * own_b, 0)[None]) / batch_total
    diag_part = jnp.sum((1.0 - corr_diag) ** 2) - redund_weight * jnp.sum(corr_diag * corr_diag)
    diag_grad = -2.0 * (1.0 - corr_diag) - 2.0 * redund_weight * corr_diag
    diag_share = (diag_part / lax.axis_size(ROWS)).reshape(1, 1)

    cols, rows, parts = gram_parts(mean, rstd, gathered, both, other, feats)
    pieces = lax.all_to_all(parts, FEAT, 0, 0)
    sent = reduce_parts(pieces, diag_share, redund_weight / (batch_total * batch_total))
    full = lax.all_to_all(sent, FEAT, 0, 0)
    coupling = 2.0 * redund_weight / (batch_total * batch_total)
    mine, leaving, sums = products(full, cols, rows, diag_grad, coupling, batch_total)
    sums, leaving = lax.optimization_barrier((pair_sum(sums), leaving))
    received = lax.ppermute(leaving, "yh", SWAP)
    back = spread(sums)
    scale = batch_total * batch_total / (redund_weight * WIDTH)
    grad_a, grad_b, loss = finish(back, rstd, mine, received, rows, scale, batch_total)
    return grad_a, grad_b, loss[0, 0]


def solution(mesh):
    fine = Mesh(mesh.devices.reshape(8, 2, 2, 2, 4), ROWS + FEAT)
    return jax.shard_map(
        shards,
        mesh=fine,
        in_specs=(P(ROWS, FEAT), P(ROWS, FEAT)),
        out_specs=(P(ROWS, FEAT), P(ROWS, FEAT), P()),
        check_vma=False,
    )
```

```python
import jax
import jax.numpy as jnp
from jax import lax
from jax.experimental import pallas as pl
from jax.experimental.pallas import tpu as pltpu
from jax.sharding import Mesh, PartitionSpec as P

WIDTH = 8192

redund_weight = 0.0051
eps_var = 1e-05

ROWS = ("z", "yh", "c")
FEAT = ("yl", "x")
SWAP = [(0, 1), (1, 0)]
LIMIT = 32 * 1024 * 1024
VMEM = pl.BlockSpec(memory_space=pltpu.VMEM)
ANY = pl.BlockSpec(memory_space=pl.ANY)


def partner(values, axis):
    return lax.ppermute(values, axis, SWAP)


def shift(values, steps):
    count = lax.axis_size("z")
    return lax.ppermute(values, "z", [(k, (k + steps) % count) for k in range(count)])


def spread(values):
    count = lax.axis_size("z")
    return lax.all_to_all(jnp.broadcast_to(values[None], (count,) + values.shape), "z", 0, 0)


def standardize(values, mean, rstd):
    return ((values.astype(jnp.float32) - mean) * rstd).astype(jnp.bfloat16)


def start_kernel(view_a, view_b, both, moments):
    for v, view in enumerate((view_a, view_b)):
        values = view[...]
        both[v] = values
        floats = values.astype(jnp.float32)
        moments[v : v + 1] = jnp.sum(floats, 0, keepdims=True)
        moments[v + 2 : v + 3] = jnp.sum(floats * floats, 0, keepdims=True)


def start(view_a, view_b):
    return pl.pallas_call(
        start_kernel,
        in_specs=[VMEM] * 2,
        out_specs=[VMEM] * 2,
        out_shape=[
            jax.ShapeDtypeStruct((2,) + view_a.shape, view_a.dtype),
            jax.ShapeDtypeStruct((4, view_a.shape[1]), jnp.float32),
        ],
        compiler_params=pltpu.CompilerParams(vmem_limit_bytes=LIMIT),
        name="start",
    )(view_a, view_b)


def moments_kernel(far, *refs):
    before, *blocks = refs[:-1]
    moments = refs[-1]
    if far:
        moments[...] = before[...] + blocks.pop(0)[...]
    else:
        moments[...] = before[...]
    for block in blocks:
        for v in range(2):
            floats = block[v].astype(jnp.float32)
            moments[v : v + 1] += jnp.sum(floats, 0, keepdims=True)
            moments[v + 2 : v + 3] += jnp.sum(floats * floats, 0, keepdims=True)


def add_moments(before, blocks, far=None):
    given = [before] + ([] if far is None else [far]) + list(blocks)
    return pl.pallas_call(
        lambda *refs: moments_kernel(far is not None, *refs),
        in_specs=[VMEM] * len(given),
        out_specs=VMEM,
        out_shape=jax.ShapeDtypeStruct(before.shape, jnp.float32),
        compiler_params=pltpu.CompilerParams(vmem_limit_bytes=LIMIT),
        name="moments",
    )(*given)


def gram_kernel(total_rows, near, far, own, other, *refs):
    blocks = refs[:-5]
    cols, rows, parts, cross, rstd = refs[-5:]
    count = own.shape[1]
    feats, _, piece, _ = parts.shape
    sums = (near[...] + far[...]) * (1.0 / total_rows)
    mean = sums[:2]
    scale = lax.rsqrt(sums[2:] - mean * mean + eps_var)
    rstd[...] = scale
    for v in range(2):
        rows[v, :count] = standardize(own[v], mean[v : v + 1], scale[v : v + 1])
        rows[v, count:] = standardize(other[v], mean[v : v + 1], scale[v : v + 1])
    products = jnp.zeros(cross.shape, jnp.float32)
    flat = iter(blocks)
    place = 0
    while place < cols.shape[1]:
        first = place
        while place < first + 2 * piece:
            pair = [next(flat)]
            if pair[0].shape[0] == 1:
                pair.append(next(flat))
            values = [
                standardize(pair[v if len(pair) == 2 else 0][v if len(pair) == 1 else 0],
                            mean[v : v + 1], scale[v : v + 1])
                for v in range(2)
            ]
            for v in range(2):
                cols[v, place : place + count] = values[v]
            products = products + jnp.sum(
                values[0].astype(jnp.float32) * values[1].astype(jnp.float32), 0, keepdims=True
            )
            place += count
        for v in range(2):
            gram = lax.dot_general(
                cols[v, first:place],
                rows[v],
                (((1,), (1,)), ((), ())),
                preferred_element_type=jnp.float32,
            )
            parts[first // piece : place // piece, v] = gram.astype(jnp.bfloat16).reshape(
                2, piece, 2 * count
            )
    cross[...] = products


def gram_parts(near, far, own, other, blocks, feats, total_rows):
    _, count, width = own.shape
    panel = count * sum(block.shape[0] for block in blocks) // 2
    return pl.pallas_call(
        lambda *refs: gram_kernel(total_rows, *refs),
        in_specs=[VMEM] * (4 + len(blocks)),
        out_specs=[VMEM] * 5,
        out_shape=[
            jax.ShapeDtypeStruct((2, panel, width), jnp.bfloat16),
            jax.ShapeDtypeStruct((2, 2 * count, width), jnp.bfloat16),
            jax.ShapeDtypeStruct((feats, 2, panel // feats, 2 * count), jnp.bfloat16),
            jax.ShapeDtypeStruct((1, width), jnp.float32),
            jax.ShapeDtypeStruct((2, width), jnp.float32),
        ],
        compiler_params=pltpu.CompilerParams(vmem_limit_bytes=LIMIT),
        name="gram",
    )(near, far, own, other, *blocks)


def reduce_kernel(weight, total_rows, share, near, far, pieces, sent, diag_grad):
    feats, _, piece, row_count = pieces.shape
    corr = (near[...] + far[...]) * (1.0 / total_rows)
    miss = 1.0 - corr
    diag_grad[...] = -2.0 * miss - 2.0 * redund_weight * corr
    diag = jnp.sum(miss * miss - redund_weight * (corr * corr), keepdims=True) * share
    total = []
    for v in range(2):
        total.append(pieces[0, v].astype(jnp.float32))
        for w in range(1, feats):
            total[v] = total[v] + pieces[w, v].astype(jnp.float32)
    frob = jnp.sum(total[0] * total[1], keepdims=True)
    part = jnp.broadcast_to(diag + weight * frob, (16, piece))
    high = part.astype(jnp.bfloat16).astype(jnp.float32)
    middle = (part - high).astype(jnp.bfloat16).astype(jnp.float32)
    low = part - high - middle
    lane = lax.broadcasted_iota(jnp.int32, part.shape, 1)
    extra = jnp.where(lane == 0, high, jnp.where(lane == 1, middle, jnp.where(lane == 2, low, 0.0)))
    extra = extra.astype(jnp.bfloat16)
    for v in range(2):
        low_gram = total[v].T.astype(jnp.bfloat16)
        for w in range(feats):
            sent[w, v, :row_count] = low_gram
            sent[w, v, row_count:] = extra


def reduce_parts(near, far, pieces, total_rows, share):
    feats, _, piece, row_count = pieces.shape
    weight = redund_weight / (total_rows * total_rows)
    return pl.pallas_call(
        lambda *refs: reduce_kernel(weight, total_rows, share, *refs),
        in_specs=[VMEM] * 3,
        out_specs=[VMEM] * 2,
        out_shape=[
            jax.ShapeDtypeStruct((feats, 2, row_count + 16, piece), jnp.bfloat16),
            jax.ShapeDtypeStruct(near.shape, jnp.float32),
        ],
        compiler_params=pltpu.CompilerParams(vmem_limit_bytes=LIMIT),
        name="reduce",
    )(near, far, pieces)


def product_kernel(coupling, total_rows, full, cols, rows, diag_grad, mine, sent, sums):
    feats, _, _, piece = full.shape
    count = rows.shape[1] // 2
    width = cols.shape[2]
    chunk = 512
    for v in range(2):
        for f in range(0, width, chunk):
            here = slice(f, f + chunk)
            product = None
            for w in range(feats):
                term = jnp.dot(
                    full[w, 1 - v, : 2 * count],
                    cols[v, w * piece : (w + 1) * piece, here],
                    preferred_element_type=jnp.float32,
                )
                product = term if product is None else product + term
            product = coupling * product
            near = product[:count] + diag_grad[:, here] * (
                rows[1 - v, :count, here].astype(jnp.float32) * (1.0 / total_rows)
            )
            far = product[count:]
            mine[v, :, here] = near
            sent[v, :, here] = far.astype(jnp.bfloat16)
            plain = jnp.sum(near, 0, keepdims=True) + jnp.sum(far, 0, keepdims=True)
            cross = jnp.sum(
                near * rows[v, :count, here].astype(jnp.float32), 0, keepdims=True
            ) + jnp.sum(far * rows[v, count:, here].astype(jnp.float32), 0, keepdims=True)
            for k in range(chunk // 128):
                row = 2 * v * (width // 128) + f // 128 + k
                sums[row : row + 1] = plain[:, k * 128 : (k + 1) * 128]
                row += width // 128
                sums[row : row + 1] = cross[:, k * 128 : (k + 1) * 128]
    pieces = full[:, 0, 2 * count : 2 * count + 16, :128].astype(jnp.float32)
    loss = jnp.sum(pieces[:, 0:1, :].reshape(feats, 128), keepdims=True)
    last = 4 * (width // 128)
    sums[last : last + 8] = jnp.broadcast_to(loss, (8, 128))


def products(full, cols, rows, diag_grad, coupling, total_rows):
    _, _, width = cols.shape
    count = rows.shape[1] // 2
    return pl.pallas_call(
        lambda *refs: product_kernel(coupling, total_rows, *refs),
        in_specs=[VMEM] * 4,
        out_specs=[VMEM] * 3,
        out_shape=[
            jax.ShapeDtypeStruct((2, count, width), jnp.float32),
            jax.ShapeDtypeStruct((2, count, width), jnp.bfloat16),
            jax.ShapeDtypeStruct((4 * (width // 128) + 8, 128), jnp.float32),
        ],
        compiler_params=pltpu.CompilerParams(vmem_limit_bytes=LIMIT),
        name="products",
    )(full, cols, rows, diag_grad)


def final_kernel(scale, total_rows, parts, rstd, mine, received, rows, grad_a, grad_b, loss):
    total = parts[0]
    for k in range(1, parts.shape[0]):
        total = total + parts[k]
    total = total * (1.0 / total_rows)
    _, count, width = mine.shape
    lanes = width // 128
    for v, out in ((0, grad_a), (1, grad_b)):
        for k in range(lanes):
            here = slice(k * 128, (k + 1) * 128)
            plain = 2 * v * lanes + k
            cross = plain + lanes
            out[:, here] = (
                (scale * rstd[v : v + 1, here])
                * (
                    mine[v, :, here]
                    + received[v, :, here].astype(jnp.float32)
                    - total[plain : plain + 1]
                    - rows[v, :count, here].astype(jnp.float32) * total[cross : cross + 1]
                )
            ).astype(jnp.bfloat16)
    loss[...] = total[4 * lanes : 4 * lanes + 1] * total_rows


def finish(parts, rstd, mine, received, rows, scale, total_rows):
    _, count, width = mine.shape
    return pl.pallas_call(
        lambda *refs: final_kernel(scale, total_rows, *refs),
        in_specs=[VMEM] * 5,
        out_specs=[VMEM] * 3,
        out_shape=[
            jax.ShapeDtypeStruct((count, width), jnp.bfloat16),
            jax.ShapeDtypeStruct((count, width), jnp.bfloat16),
            jax.ShapeDtypeStruct((1, 128), jnp.float32),
        ],
        compiler_params=pltpu.CompilerParams(vmem_limit_bytes=LIMIT),
        name="finish",
    )(parts, rstd, mine, received, rows)


def shards(view_a, view_b):
    row_count, _ = view_a.shape
    batch_total = row_count * lax.axis_size(ROWS)
    feats = lax.axis_size(FEAT)
    both, sums = start(view_a, view_b)

    right = left = both
    blocks = [[both]]
    other = partner(both, "yh")
    opposite = shift(sums, lax.axis_size("z") // 2)
    for _ in range(lax.axis_size("z") // 2 - 1):
        right, left = shift(right, 1), shift(left, -1)
        blocks += [[right], [left]]
        sums = add_moments(sums, (right, left), opposite if len(blocks) == 7 else None)
    blocks.append([shift(right[:1], 1), shift(left[1:], -1)])
    flat = []
    for block in blocks:
        flat += block + [partner(half, "c") for half in block]
    sums = sums + partner(sums, "c")
    cols, rows, parts, cross, rstd = gram_parts(
        sums, partner(sums, "yh"), both, other, flat, feats, batch_total
    )
    cross_far = partner(cross, "yh")
    pieces = lax.all_to_all(parts, FEAT, 0, 0)
    sent, diag_grad = reduce_parts(
        cross, cross_far, pieces, batch_total, 1.0 / lax.axis_size(ROWS)
    )
    full = lax.all_to_all(sent, FEAT, 0, 0)
    coupling = 2.0 * redund_weight / (batch_total * batch_total)
    mine, leaving, sums = products(full, cols, rows, diag_grad, coupling, batch_total)
    sums = sums + partner(sums, "c")
    sums, leaving = lax.optimization_barrier((sums + partner(sums, "yh"), leaving))
    received = partner(leaving, "yh")
    back = spread(sums)
    scale = batch_total * batch_total / (redund_weight * WIDTH)
    grad_a, grad_b, loss = finish(back, rstd, mine, received, rows, scale, batch_total)
    return grad_a, grad_b, loss[0, 0]


def solution(mesh):
    fine = Mesh(mesh.devices.reshape(8, 2, 2, 2, 4), ROWS + FEAT)
    return jax.shard_map(
        shards,
        mesh=fine,
        in_specs=(P(ROWS, FEAT), P(ROWS, FEAT)),
        out_specs=(P(ROWS, FEAT), P(ROWS, FEAT), P()),
        check_vma=False,
    )
```

```python
import jax
import jax.numpy as jnp
from jax import lax
from jax.experimental import pallas as pl
from jax.experimental.pallas import tpu as pltpu
from jax.sharding import Mesh, PartitionSpec as P

WIDTH = 8192

redund_weight = 0.0051
eps_var = 1e-05

ROWS = ("z", "yh", "c")
FEAT = ("yl", "x")
SWAP = [(0, 1), (1, 0)]
LIMIT = 32 * 1024 * 1024
VMEM = pl.BlockSpec(memory_space=pltpu.VMEM)
ANY = pl.BlockSpec(memory_space=pl.ANY)
SMEM = pl.BlockSpec(memory_space=pltpu.SMEM)


def partner(values, axis):
    return lax.ppermute(values, axis, SWAP)


def shift(values, steps):
    count = lax.axis_size("z")
    return lax.ppermute(values, "z", [(k, (k + steps) % count) for k in range(count)])


def quad(values):
    return [
        lax.ppermute(values, ("yh", "c"), [(k, k ^ step) for k in range(4)]) for step in (3, 2, 1)
    ]


def peers(values):
    count = lax.axis_size(FEAT)
    return {
        step: lax.ppermute(value, FEAT, [(k, k ^ step) for k in range(count)])
        for step, value in values
    }


def spread(values):
    count = lax.axis_size("z")
    return lax.all_to_all(jnp.broadcast_to(values[None], (count,) + values.shape), "z", 0, 0)


def standardize(values, mean, rstd):
    return ((values.astype(jnp.float32) - mean) * rstd).astype(jnp.bfloat16)


def start_kernel(view_a, view_b, both, moments, sems):
    copies = [
        pltpu.make_async_copy(view, both.at[v], sems.at[v])
        for v, view in enumerate((view_a, view_b))
    ]
    for copy in copies:
        copy.start()
    for v, copy in enumerate(copies):
        copy.wait()
        floats = both[v].astype(jnp.float32)
        moments[v : v + 1] = jnp.sum(floats, 0, keepdims=True)
        moments[v + 2 : v + 3] = jnp.sum(floats * floats, 0, keepdims=True)


def start(view_a, view_b):
    return pl.pallas_call(
        start_kernel,
        in_specs=[ANY] * 2,
        out_specs=[VMEM] * 2,
        out_shape=[
            jax.ShapeDtypeStruct((2,) + view_a.shape, view_a.dtype),
            jax.ShapeDtypeStruct((4, view_a.shape[1]), jnp.float32),
        ],
        scratch_shapes=[pltpu.SemaphoreType.DMA((2,))],
        compiler_params=pltpu.CompilerParams(vmem_limit_bytes=LIMIT),
        name="start",
    )(view_a, view_b)


def moments_kernel(far, *refs):
    before, *blocks = refs[:-1]
    moments = refs[-1]
    if far:
        moments[...] = before[...] + blocks.pop(0)[...]
    else:
        moments[...] = before[...]
    for block in blocks:
        for v in range(2):
            floats = block[v].astype(jnp.float32)
            moments[v : v + 1] += jnp.sum(floats, 0, keepdims=True)
            moments[v + 2 : v + 3] += jnp.sum(floats * floats, 0, keepdims=True)


def add_moments(before, blocks, far=None):
    given = [before] + ([] if far is None else [far]) + list(blocks)
    return pl.pallas_call(
        lambda *refs: moments_kernel(far is not None, *refs),
        in_specs=[VMEM] * len(given),
        out_specs=VMEM,
        out_shape=jax.ShapeDtypeStruct(before.shape, jnp.float32),
        compiler_params=pltpu.CompilerParams(vmem_limit_bytes=LIMIT),
        name="moments",
    )(*given)


def gram_kernel(total_rows, count_parts, me, *refs):
    sums = refs[:4]
    own, other = refs[4:6]
    blocks = refs[6 : -count_parts - 4]
    parts = refs[-count_parts - 4 : -4]
    cols, rows, cross, rstd = refs[-4:]
    count = own.shape[1]
    piece = cols.shape[1] // count_parts
    moments = (sums[0][...] + sums[1][...] + sums[2][...] + sums[3][...]) * (1.0 / total_rows)
    mean = moments[:2]
    scale = lax.rsqrt(moments[2:] - mean * mean + eps_var)
    rstd[...] = scale
    for v in range(2):
        rows[v, :count] = standardize(own[v], mean[v : v + 1], scale[v : v + 1])
        rows[v, count:] = standardize(other[v], mean[v : v + 1], scale[v : v + 1])
    products = jnp.zeros(cross.shape, jnp.float32)
    flat = iter(blocks)
    for place in range(0, cols.shape[1], count):
        block = next(flat)
        pair = [block.at[0], block.at[1]] if block.shape[0] == 2 else [block.at[0], next(flat).at[0]]
        values = [
            standardize(pair[v][...], mean[v : v + 1], scale[v : v + 1]) for v in range(2)
        ]
        for v in range(2):
            cols[v, place : place + count] = values[v]
        products = products + jnp.sum(
            values[0].astype(jnp.float32) * values[1].astype(jnp.float32), 0, keepdims=True
        )
    cross[...] = products
    for step, part in enumerate(parts):
        first = pl.multiple_of((me[0] ^ step) * piece, piece)
        for v in range(2):
            gram = lax.dot_general(
                cols[v, pl.ds(first, piece)],
                rows[v],
                (((1,), (1,)), ((), ())),
                preferred_element_type=jnp.float32,
            )
            part[v] = gram.astype(jnp.bfloat16)


def gram_parts(me, sums, own, other, blocks, feats, total_rows):
    _, count, width = own.shape
    panel = count * sum(block.shape[0] for block in blocks) // 2
    out = pl.pallas_call(
        lambda *refs: gram_kernel(total_rows, feats, *refs),
        in_specs=[SMEM] + [VMEM] * (6 + len(blocks)),
        out_specs=[VMEM] * (feats + 4),
        out_shape=[jax.ShapeDtypeStruct((2, panel // feats, 2 * count), jnp.bfloat16)] * feats
        + [
            jax.ShapeDtypeStruct((2, panel, width), jnp.bfloat16),
            jax.ShapeDtypeStruct((2, 2 * count, width), jnp.bfloat16),
            jax.ShapeDtypeStruct((1, width), jnp.float32),
            jax.ShapeDtypeStruct((2, width), jnp.float32),
        ],
        compiler_params=pltpu.CompilerParams(vmem_limit_bytes=LIMIT),
        name="gram",
    )(me, *sums, own, other, *blocks)
    return out[:feats], *out[feats:]


def reduce_kernel(weight, total_rows, share, near, far, *refs):
    pieces = refs[:-2]
    sent, diag_grad = refs[-2:]
    _, piece, row_count = pieces[0].shape
    corr = (near[...] + far[...]) * (1.0 / total_rows)
    miss = 1.0 - corr
    diag_grad[...] = -2.0 * miss - 2.0 * redund_weight * corr
    diag = jnp.sum(miss * miss - redund_weight * (corr * corr), keepdims=True) * share
    total = []
    for v in range(2):
        total.append(pieces[0][v].astype(jnp.float32))
        for other in pieces[1:]:
            total[v] = total[v] + other[v].astype(jnp.float32)
    frob = jnp.sum(total[0] * total[1], keepdims=True)
    part = jnp.broadcast_to(diag + weight * frob, (16, piece))
    high = part.astype(jnp.bfloat16).astype(jnp.float32)
    middle = (part - high).astype(jnp.bfloat16).astype(jnp.float32)
    low = part - high - middle
    lane = lax.broadcasted_iota(jnp.int32, part.shape, 1)
    extra = jnp.where(lane == 0, high, jnp.where(lane == 1, middle, jnp.where(lane == 2, low, 0.0)))
    for v in range(2):
        sent[v, :row_count] = total[v].T.astype(jnp.bfloat16)
        sent[v, row_count:] = extra.astype(jnp.bfloat16)


def reduce_parts(near, far, pieces, total_rows, share):
    _, piece, row_count = pieces[0].shape
    weight = redund_weight / (total_rows * total_rows)
    return pl.pallas_call(
        lambda *refs: reduce_kernel(weight, total_rows, share, *refs),
        in_specs=[VMEM] * (2 + len(pieces)),
        out_specs=[VMEM] * 2,
        out_shape=[
            jax.ShapeDtypeStruct((2, row_count + 16, piece), jnp.bfloat16),
            jax.ShapeDtypeStruct(near.shape, jnp.float32),
        ],
        compiler_params=pltpu.CompilerParams(vmem_limit_bytes=LIMIT),
        name="reduce",
    )(near, far, *pieces)


def product_kernel(coupling, total_rows, me, cols, rows, diag_grad, *refs):
    full = refs[:-3]
    mine, sent, sums = refs[-3:]
    _, _, piece = full[0].shape
    count = rows.shape[1] // 2
    width = cols.shape[2]
    chunk = 512
    for v in range(2):
        for f in range(0, width, chunk):
            here = slice(f, f + chunk)
            product = None
            for step, part in enumerate(full):
                first = pl.multiple_of((me[0] ^ step) * piece, piece)
                term = jnp.dot(
                    part[1 - v, : 2 * count],
                    cols[v, pl.ds(first, piece), here],
                    preferred_element_type=jnp.float32,
                )
                product = term if product is None else product + term
            product = coupling * product
            near = product[:count] + diag_grad[:, here] * (
                rows[1 - v, :count, here].astype(jnp.float32) * (1.0 / total_rows)
            )
            far = product[count:]
            mine[v, :, here] = near
            sent[v, :, here] = far.astype(jnp.bfloat16)
            plain = jnp.sum(near, 0, keepdims=True) + jnp.sum(far, 0, keepdims=True)
            cross = jnp.sum(
                near * rows[v, :count, here].astype(jnp.float32), 0, keepdims=True
            ) + jnp.sum(far * rows[v, count:, here].astype(jnp.float32), 0, keepdims=True)
            for k in range(chunk // 128):
                row = 2 * v * (width // 128) + f // 128 + k
                sums[row : row + 1] = plain[:, k * 128 : (k + 1) * 128]
                row += width // 128
                sums[row : row + 1] = cross[:, k * 128 : (k + 1) * 128]
    loss = jnp.zeros((16, 128), jnp.float32)
    for part in full:
        loss = loss + part[0, 2 * count : 2 * count + 16, :128].astype(jnp.float32)
    loss = jnp.sum(loss[:1], keepdims=True)
    last = 4 * (width // 128)
    sums[last : last + 8] = jnp.broadcast_to(loss, (8, 128))


def products(me, full, cols, rows, diag_grad, coupling, total_rows):
    _, _, width = cols.shape
    count = rows.shape[1] // 2
    return pl.pallas_call(
        lambda *refs: product_kernel(coupling, total_rows, *refs),
        in_specs=[SMEM] + [VMEM] * (3 + len(full)),
        out_specs=[VMEM] * 3,
        out_shape=[
            jax.ShapeDtypeStruct((2, count, width), jnp.float32),
            jax.ShapeDtypeStruct((2, count, width), jnp.bfloat16),
            jax.ShapeDtypeStruct((4 * (width // 128) + 8, 128), jnp.float32),
        ],
        compiler_params=pltpu.CompilerParams(vmem_limit_bytes=LIMIT),
        name="products",
    )(me, cols, rows, diag_grad, *full)


def final_kernel(scale, total_rows, parts, rstd, mine, received, rows, grad_a, grad_b, loss):
    total = parts[0]
    for k in range(1, parts.shape[0]):
        total = total + parts[k]
    total = total * (1.0 / total_rows)
    _, count, width = mine.shape
    lanes = width // 128
    for v, out in ((0, grad_a), (1, grad_b)):
        for k in range(lanes):
            here = slice(k * 128, (k + 1) * 128)
            plain = 2 * v * lanes + k
            cross = plain + lanes
            out[:, here] = (
                (scale * rstd[v : v + 1, here])
                * (
                    mine[v, :, here]
                    + received[v, :, here].astype(jnp.float32)
                    - total[plain : plain + 1]
                    - rows[v, :count, here].astype(jnp.float32) * total[cross : cross + 1]
                )
            ).astype(jnp.bfloat16)
    loss[...] = total[4 * lanes : 4 * lanes + 1] * total_rows


def finish(parts, rstd, mine, received, rows, scale, total_rows):
    _, count, width = mine.shape
    return pl.pallas_call(
        lambda *refs: final_kernel(scale, total_rows, *refs),
        in_specs=[VMEM] * 5,
        out_specs=[VMEM] * 3,
        out_shape=[
            jax.ShapeDtypeStruct((count, width), jnp.bfloat16),
            jax.ShapeDtypeStruct((count, width), jnp.bfloat16),
            jax.ShapeDtypeStruct((1, 128), jnp.float32),
        ],
        compiler_params=pltpu.CompilerParams(vmem_limit_bytes=LIMIT),
        name="finish",
    )(parts, rstd, mine, received, rows)


def shards(view_a, view_b):
    row_count, _ = view_a.shape
    batch_total = row_count * lax.axis_size(ROWS)
    feats = lax.axis_size(FEAT)
    both, sums = start(view_a, view_b)

    right = left = both
    blocks = [[both]]
    other = partner(both, "yh")
    opposite = shift(sums, lax.axis_size("z") // 2)
    for _ in range(lax.axis_size("z") // 2 - 1):
        right, left = shift(right, 1), shift(left, -1)
        blocks += [[right], [left]]
        sums = add_moments(sums, (right, left), opposite if len(blocks) == 7 else None)
    blocks.append([shift(right[:1], 1), shift(left[1:], -1)])
    flat = []
    for block in blocks:
        flat += block + [partner(half, "c") for half in block]
    me = lax.axis_index(FEAT).astype(jnp.int32).reshape(1)
    parts, cols, rows, cross, rstd = gram_parts(
        me, [sums] + quad(sums), both, other, flat, feats, batch_total
    )
    order = [7, 6, 5, 4, 3, 2, 1][: feats - 1]
    cross_far = partner(cross, "yh")
    come = peers([(step, parts[step]) for step in order])
    sent, diag_grad = reduce_parts(
        cross,
        cross_far,
        [parts[0]] + [come[step] for step in range(1, feats)],
        batch_total,
        1.0 / lax.axis_size(ROWS),
    )
    come = peers([(step, sent) for step in order])
    full = [sent] + [come[step] for step in range(1, feats)]
    coupling = 2.0 * redund_weight / (batch_total * batch_total)
    mine, leaving, sums = products(me, full, cols, rows, diag_grad, coupling, batch_total)
    near = quad(sums)
    sums, leaving = lax.optimization_barrier((sums + near[0] + near[1] + near[2], leaving))
    received = partner(leaving, "yh")
    back = spread(sums)
    scale = batch_total * batch_total / (redund_weight * WIDTH)
    grad_a, grad_b, loss = finish(back, rstd, mine, received, rows, scale, batch_total)
    return grad_a, grad_b, loss[0, 0]


def solution(mesh):
    fine = Mesh(mesh.devices.reshape(8, 2, 2, 2, 4), ROWS + FEAT)
    return jax.shard_map(
        shards,
        mesh=fine,
        in_specs=(P(ROWS, FEAT), P(ROWS, FEAT)),
        out_specs=(P(ROWS, FEAT), P(ROWS, FEAT), P()),
        check_vma=False,
    )
```

```python
import jax
import jax.numpy as jnp
from jax import lax
from jax.experimental import pallas as pl
from jax.experimental.pallas import tpu as pltpu
from jax.sharding import Mesh, PartitionSpec as P

WIDTH = 8192

redund_weight = 0.0051
eps_var = 1e-05

ROWS = ("z", "yh", "c")
FEAT = ("yl", "x")
RING = ("yh", "yl")
LIMIT = 24 * 1024 * 1024
VMEM = pl.BlockSpec(memory_space=pltpu.VMEM)
SMEM = pl.BlockSpec(memory_space=pltpu.SMEM)
f32 = jnp.float32
bf16 = jnp.bfloat16


def shape(*dims, dtype=f32):
    return jax.ShapeDtypeStruct(dims, dtype)


def call(kernel, name, ids, args, outs, scratch=(), aliases=(), flops=0):
    return pl.pallas_call(
        kernel,
        in_specs=[SMEM] + [VMEM] * len(args),
        out_specs=[VMEM] * len(outs),
        out_shape=outs,
        scratch_shapes=list(scratch),
        input_output_aliases=dict(aliases),
        cost_estimate=pl.CostEstimate(flops=flops, bytes_accessed=0, transcendentals=0),
        compiler_params=pltpu.CompilerParams(vmem_limit_bytes=LIMIT),
        name=name,
    )(ids, *args)


def swap(values, axes, step):
    count = lax.axis_size(axes)
    return lax.ppermute(values, axes, [(k, k ^ step) for k in range(count)])


def shift(values, steps):
    count = lax.axis_size("z")
    return lax.ppermute(values, "z", [(k, (k + steps) % count) for k in range(count)])


def exchange_sum(values, axes, steps):
    for step in steps:
        values = values + swap(values, axes, step)
    return values


def tie(values, *others):
    return lax.optimization_barrier((values, others))[0]


def standardize(values, mean, rstd):
    return ((values.astype(f32) - mean) * rstd).astype(bf16)


def column_sum(values):
    return jnp.sum(values, 0, keepdims=True)


def flat_rows(block):
    return block[...].reshape(-1, block.shape[-1])


def split_kernel(ids, keep, got, near, rest, whole):
    c, yl = ids[0], ids[1]
    half = keep.shape[0] // 2
    for k, place in enumerate((yl, 1 - yl)):
        here = pl.ds(pl.multiple_of(place * half, half), half)
        out = near if k == 0 else rest
        out[c] = keep[here]
        out[1 - c] = got[here]
        whole[2 * k : 2 * k + 2] = out[...]


def moments_kernel(given, ids, *refs):
    moments = refs[-1]
    before, blocks = refs[:given], refs[given:-1]
    total = None
    for ref in before:
        total = ref[...] if total is None else total + ref[...]
    rows = [None] * 4
    for k, block in enumerate(blocks):
        floats = flat_rows(block).astype(f32)
        place = 0 if k < len(blocks) // 2 else 2
        for j, term in enumerate((column_sum(floats), column_sum(floats * floats))):
            rows[place + j] = term if rows[place + j] is None else rows[place + j] + term
    for j in range(4):
        moments[j : j + 1] = rows[j] if total is None else rows[j] + total[j : j + 1]


def add_moments(ids, before, near, far):
    width = near[0].shape[-1]
    return call(
        lambda *refs: moments_kernel(len(before), *refs),
        "moments",
        ids,
        [*before, *near, *far],
        [shape(4, width)],
    )[0]


def fill_columns(cols, place, blocks, stats):
    for half, sources in enumerate(blocks):
        width = stats.shape[1]
        first = place
        for source in sources:
            size = source.shape[0] * source.shape[1]
            cols[first : first + size, half * width : (half + 1) * width] = standardize(
                flat_rows(source), stats[2 * half : 2 * half + 1], stats[2 * half + 1 : 2 * half + 2]
            )
            first += size
    return first


def inner(left, right):
    return lax.dot_general(
        left, right, (((1,), (1,)), ((), ())), preferred_element_type=f32
    ).astype(bf16)


def gram_kernel(total_rows, blocks, ids, *refs):
    mine, one, two, three = refs[:4]
    near, rest, near_whole, far, far_rest, far_whole = refs[4:10]
    streams = refs[10 : 10 + blocks], refs[10 + blocks : 10 + 2 * blocks]
    pieces, cols, rows, stats = refs[-4:]
    yl = ids[1]
    width = mine.shape[1]
    own = mine[...] + two[...]
    cross = one[...] + three[...]
    for half in range(2):
        sums = [
            own[2 * half + j : 2 * half + j + 1] + cross[2 - 2 * half + j : 3 - 2 * half + j]
            for j in range(2)
        ]
        mean = sums[0] * (1.0 / total_rows)
        stats[2 * half : 2 * half + 1] = mean
        stats[2 * half + 1 : 2 * half + 2] = lax.rsqrt(
            sums[1] * (1.0 / total_rows) - mean * mean + eps_var
        )
    count = rows.shape[0] // 4
    sources = (
        (near.at[0:2], rest.at[0:2], near_whole.at[0:2], near_whole.at[2:4]),
        (far.at[0:2], far_rest.at[0:2], far_whole.at[2:4], far_whole.at[0:2]),
    )
    for half in range(2):
        for k, source in enumerate(sources[half]):
            place = yl if k % 2 == 0 else 1 - yl
            first = pl.multiple_of((k // 2) * 2 * count + place * count, count)
            rows[pl.ds(first, count), half * width : (half + 1) * width] = standardize(
                flat_rows(source), stats[2 * half : 2 * half + 1], stats[2 * half + 1 : 2 * half + 2]
            )
    last = fill_columns(cols, 0, streams, stats)
    piece = pieces.shape[1]
    for first in range(0, last, piece):
        pieces[first // piece] = inner(cols[first : first + piece], rows[...])


def last_gram_kernel(blocks, ids, stats, rows, before, old, *refs):
    streams = refs[:blocks], refs[blocks : 2 * blocks]
    parts = refs[2 * blocks : -2]
    cols, pieces = refs[-2:]
    del old
    count, piece, _ = before.shape
    x = ids[2]
    fill_columns(cols, count * piece, streams, stats)
    pieces[count ^ x] = inner(cols[count * piece :], rows[...])
    for k in range(count):
        pieces[k ^ x] = before[k]
    for k, part in enumerate(parts):
        part[...] = pieces[k]


def reduce_kernel(ids, *refs):
    total = refs[0][...].astype(f32)
    for ref in refs[1:-2]:
        total = total + ref[...].astype(f32)
    flipped = total.T
    refs[-2][...] = flipped.astype(bf16)
    refs[-1][...] = flipped


def native_kernel(ids, view_a, view_b, mine, theirs, norm, rstd, sums):
    c = ids[0]
    values = []
    for v, view in enumerate((view_a, view_b)):
        stats = jnp.where(c == v, mine[...], theirs[...])
        rstd[v : v + 1] = stats[1:2]
        rounded = standardize(view[...], stats[0:1], stats[1:2])
        norm[v] = rounded
        values.append(rounded.astype(f32))
        sums[v : v + 1] = column_sum(values[v])
    sums[2:3] = column_sum(values[0] * values[1])
    sums[3:4] = jnp.zeros_like(rstd[0:1])


def diagonal(totals, total_rows):
    corr = totals[2:3] * (1.0 / total_rows)
    return corr, -2.0 * (1.0 - corr) - 2.0 * redund_weight * corr


def loss_kernel(total_rows, share, ids, gram, other, totals, loss):
    corr, _ = diagonal(totals[...], total_rows)
    miss = 1.0 - corr
    diag = jnp.sum(miss * miss - redund_weight * (corr * corr), keepdims=True)
    frob = jnp.sum(gram[...] * other[...].astype(f32), keepdims=True)
    weight = 0.5 * redund_weight / (total_rows * total_rows)
    loss[...] = jnp.broadcast_to(share * diag + weight * frob, loss.shape)


def product_kernel(coupling, side, count_full, ids, *refs):
    full = refs[:count_full]
    cols, rows = refs[count_full : count_full + 2]
    targets = refs[count_full + 2 : -2]
    sums, scratch = refs[-2:]
    c, x = ids[0], ids[2]
    piece = full[0].shape[1]
    count, width = targets[0].shape
    half = count // 2
    chunk = scratch.shape[1]
    lanes = width // 128
    for local in range(0, width, chunk):
        here = slice(side * width + local, side * width + local + chunk)
        product = None
        for step, part in enumerate(full):
            first = pl.multiple_of((x ^ step) * piece, piece)
            term = jnp.dot(part[...], cols[pl.ds(first, piece), here], preferred_element_type=f32)
            product = term if product is None else product + term
        product = coupling * product
        scratch[...] = product
        plain = column_sum(product)
        cross = column_sum(product * rows[:, here].astype(f32))
        for k in range(chunk // 128):
            row = local // 128 + k
            sums[row : row + 1] = plain[:, k * 128 : (k + 1) * 128]
            sums[lanes + row : lanes + row + 1] = cross[:, k * 128 : (k + 1) * 128]
        for place, target in enumerate(targets):
            for h in range(2):
                first = (place // 2) * 2 * count + h * count + (c ^ (place % 2)) * half
                values = scratch[pl.ds(pl.multiple_of(first, half), half)]
                target[h * half : (h + 1) * half, local : local + chunk] = values.astype(
                    target.dtype
                )


def final_kernel(scale, total_rows, ids, ours, theirs, totals, rstd, norm, mine, *refs):
    come, (grad_a, grad_b) = refs[:-2], refs[-2:]
    c = ids[0]
    count, width = mine.shape
    lanes = width // 128
    back = [jnp.where(c == v, ours[...], theirs[...]) for v in range(2)]
    _, diag_grad = diagonal(totals[...], total_rows)
    diag_grad = diag_grad * (1.0 / total_rows)
    for k in range(lanes):
        here = slice(k * 128, (k + 1) * 128)
        same, cross = mine[:, here], None
        for place, ref in enumerate(come, 1):
            values = ref[:, here].astype(f32)
            if place & 2:
                cross = values if cross is None else cross + values
            else:
                same = same + values
        for v, out in enumerate((grad_a, grad_b)):
            weight = diag_grad[:, here]
            mean_grad = back[v][k : k + 1] + weight * totals[1 - v : 2 - v, here]
            mean_cross = back[v][lanes + k : lanes + k + 1] + weight * totals[2:3, here]
            grad = jnp.where(c == v, same, cross) + weight * norm[1 - v, :, here].astype(f32)
            out[:, here] = (
                (scale * rstd[v : v + 1, here])
                * (
                    grad
                    - mean_grad * (1.0 / total_rows)
                    - norm[v, :, here].astype(f32) * (mean_cross * (1.0 / total_rows))
                )
            ).astype(bf16)


def shards(view_a, view_b):
    count, width = view_a.shape
    total_rows = count * lax.axis_size(ROWS)
    places = [lax.axis_index(name) for name in ("c", "yl", "x")]
    ids = jnp.stack(places).astype(jnp.int32)
    half = count // 2
    block = shape(2, half, width, dtype=bf16)
    hops = lax.axis_size("z") // 2
    peers = lax.axis_size("x")

    first = places[0] == 0
    keep, give = jnp.where(first, view_a, view_b), jnp.where(first, view_b, view_a)
    near, rest, whole = call(
        split_kernel,
        "split",
        ids,
        [keep, swap(give, "c", 1)],
        [block, block, shape(4, half, width, dtype=bf16)],
    )

    far = swap(rest, RING, 1)
    whole_far, near_far, whole_near = swap(whole, RING, 3), swap(near, RING, 1), swap(whole, RING, 2)
    streams = [[near], [far]]
    ends = [[near, near], [far, far]]
    moments = add_moments(ids, [], [near], [far])
    opposite = shift(moments, hops)
    before = {3: ([], [whole_far]), 4: ([moments, near_far], [whole_near])}
    for hop in range(1, hops + 1):
        for k, (stream, end) in enumerate(zip(streams, ends)):
            if before.get(hop, ([], []))[k]:
                end[0], end[1] = tie((end[0], end[1]), *before[hop][k])
            if hop < hops:
                end[:] = [shift(end[0], 1), shift(end[1], -1)]
                stream += end
            else:
                stream += [shift(end[0][:1], 1), shift(end[1][1:], -1)]
        if hop < hops:
            moments = add_moments(
                ids, [moments] + ([opposite] if hop == hops - 1 else []), ends[0], ends[1]
            )
        if hop == 2:
            before[4] = ([moments, near_far], [whole_near])
    row_blocks = [near, rest, whole_near, far, near_far, whole_far]
    panel = 2 * half * lax.axis_size("z")
    piece = panel // peers
    early = 2 * (peers - 1)
    pieces, cols, rows, stats = call(
        lambda *refs: gram_kernel(total_rows, early, *refs),
        "gram",
        ids,
        [moments] + [swap(moments, RING, k) for k in (1, 2, 3)] + row_blocks
        + streams[0][:early] + streams[1][:early],
        [
            shape(peers - 1, piece, 4 * count, dtype=bf16),
            shape(panel, 2 * width, dtype=bf16),
            shape(4 * count, 2 * width, dtype=bf16),
            shape(4, width),
        ],
        flops=4 * count * panel * width * 3,
    )
    late = len(streams[0]) - early
    *parts, cols = call(
        lambda *refs: last_gram_kernel(late, *refs),
        "last_gram",
        ids,
        [stats, rows, pieces, cols] + streams[0][early:] + streams[1][early:],
        [shape(piece, 4 * count, dtype=bf16)] * peers + [shape(panel, 2 * width, dtype=bf16)],
        [pltpu.VMEM((peers, piece, 4 * count), bf16)],
        {4: peers},
    )

    come = [swap(parts[k], ("c", "x"), peers | k) for k in range(peers)]
    norm, rstd, sums = call(
        native_kernel,
        "native",
        ids,
        [view_a, view_b, stats[:2], swap(stats[:2], "c", 1)],
        [shape(2, count, width, dtype=bf16), shape(2, width), shape(4, width)],
    )
    sums = exchange_sum(sums, "c", (1,))
    sums = exchange_sum(sums, "yh", (1,))
    come[0] = tie(come[0], sums)
    low_gram, gram = call(
        reduce_kernel,
        "reduce",
        ids,
        come,
        [shape(4 * count, piece, dtype=bf16), shape(4 * count, piece)],
    )
    full = [low_gram] + [swap(low_gram, "x", k) for k in range(1, peers)]
    totals = exchange_sum(sums, "z", (1, 2, 4))
    loss = call(
        lambda *refs: loss_kernel(total_rows, 1.0 / lax.axis_size(ROWS), *refs),
        "loss",
        ids,
        [gram, swap(low_gram, "c", 1), totals],
        [shape(8, 128)],
    )[0]

    lanes = width // 128

    def product(side, dtypes):
        return call(
            lambda *refs: product_kernel(
                2.0 * redund_weight / (total_rows * total_rows), side, peers, *refs
            ),
            "products",
            ids,
            full + [cols, rows],
            [shape(count, width, dtype=dtype) for dtype in dtypes] + [shape(2 * lanes, 128)],
            [pltpu.VMEM((4 * count, width // 2), f32)],
            flops=8 * count * panel * width,
        )

    leaving = {}
    leaving[1], leaving[3], leaving[5], leaving[7], far_sums = product(1, [bf16] * 4)
    mine, leaving[2], leaving[4], leaving[6], near_sums = product(0, [f32] + [bf16] * 3)
    come = {k: swap(leaving[k], ("yh", "c", "yl"), k) for k in (1, 5, 3, 7, 4, 6, 2)}
    near_sums = jnp.concatenate([near_sums, loss])
    far_sums = jnp.concatenate([far_sums, loss])
    back = near_sums + swap(near_sums, RING, 2) + swap(far_sums, RING, 1) + swap(far_sums, RING, 3)
    back = exchange_sum(tie(back, come[1], come[3], come[5], come[7]), "z", (1, 2))
    back = exchange_sum(tie(back, come[4], come[6]), "z", (4,))
    other = swap(back, "c", 1)
    loss = back[2 * lanes :] + other[2 * lanes :]
    loss = loss + swap(loss, "x", 1) + swap(loss, "x", 2) + swap(loss, "x", 3)
    grad_a, grad_b = call(
        lambda *refs: final_kernel(
            total_rows * total_rows / (redund_weight * WIDTH), total_rows, *refs
        ),
        "finish",
        ids,
        [back, other, totals, rstd, norm, mine] + [come[k] for k in range(1, 8)],
        [shape(count, width, dtype=bf16)] * 2,
    )
    return grad_a, grad_b, loss[0, 0]


def solution(mesh):
    fine = Mesh(mesh.devices.reshape(8, 2, 2, 2, 4), ROWS + FEAT)
    return jax.shard_map(
        shards,
        mesh=fine,
        in_specs=(P(ROWS, FEAT), P(ROWS, FEAT)),
        out_specs=(P(ROWS, FEAT), P(ROWS, FEAT), P()),
        check_vma=False,
    )
```

```python
import jax
import jax.numpy as jnp
from jax import lax
from jax.experimental import pallas as pl
from jax.experimental.pallas import tpu as pltpu
from jax.sharding import Mesh, PartitionSpec as P

WIDTH = 8192

redund_weight = 0.0051
eps_var = 1e-05

ROWS = ("z", "yh", "c")
FEAT = ("yl", "x")
RING = ("yh", "yl")
LIMIT = 24 * 1024 * 1024
VMEM = pl.BlockSpec(memory_space=pltpu.VMEM)
SMEM = pl.BlockSpec(memory_space=pltpu.SMEM)
f32 = jnp.float32
bf16 = jnp.bfloat16


def shape(*dims, dtype=f32):
    return jax.ShapeDtypeStruct(dims, dtype)


def call(kernel, name, ids, args, outs, scratch=(), aliases=(), flops=0):
    return pl.pallas_call(
        kernel,
        in_specs=[SMEM] + [VMEM] * len(args),
        out_specs=[VMEM] * len(outs),
        out_shape=outs,
        scratch_shapes=list(scratch),
        input_output_aliases=dict(aliases),
        cost_estimate=pl.CostEstimate(flops=flops, bytes_accessed=0, transcendentals=0),
        compiler_params=pltpu.CompilerParams(vmem_limit_bytes=LIMIT),
        name=name,
    )(ids, *args)


def swap(values, axes, step):
    count = lax.axis_size(axes)
    return lax.ppermute(values, axes, [(k, k ^ step) for k in range(count)])


def shift(values, steps):
    count = lax.axis_size("z")
    return lax.ppermute(values, "z", [(k, (k + steps) % count) for k in range(count)])


def exchange_sum(values, axes, steps):
    for step in steps:
        values = values + swap(values, axes, step)
    return values


def tie(values, *others):
    return lax.optimization_barrier((values, others))[0]


def standardize(values, mean, rstd):
    return ((values.astype(f32) - mean) * rstd).astype(bf16)


def column_sum(values):
    return jnp.sum(values, 0, keepdims=True)


def flat_rows(block):
    return block[...].reshape(-1, block.shape[-1])


def split_kernel(ids, keep, got, near, rest, whole):
    c, yl = ids[0], ids[1]
    half = keep.shape[0] // 2
    for k, place in enumerate((yl, 1 - yl)):
        here = pl.ds(pl.multiple_of(place * half, half), half)
        out = near if k == 0 else rest
        out[c] = keep[here]
        out[1 - c] = got[here]
        whole[2 * k : 2 * k + 2] = out[...]


def merge_kernel(ids, right_near, right_far, left_near, left_far, right, left):
    right[0:2], right[2:4] = right_near[...], right_far[...]
    left[0:2], left[2:4] = left_near[...], left_far[...]


def halves(block):
    return block.at[0:2], block.at[2:4]


def moments_kernel(given, near_count, ids, *refs):
    moments = refs[-1]
    before, blocks = refs[:given], refs[given:-1]
    if near_count == len(blocks):
        pairs = [halves(block) for block in blocks]
    else:
        pairs = list(zip(blocks[:near_count], blocks[near_count:]))
    for half in range(2):
        for j in range(2):
            row = 2 * half + j
            total = None
            for ref in before:
                term = ref[row : row + 1]
                total = term if total is None else total + term
            for pair in pairs:
                floats = flat_rows(pair[half]).astype(f32)
                term = column_sum(floats * floats if j else floats)
                total = term if total is None else total + term
            moments[row : row + 1] = total


def add_moments(ids, before, near, far):
    width = near[0].shape[-1]
    return call(
        lambda *refs: moments_kernel(len(before), len(near), *refs),
        "moments",
        ids,
        [*before, *near, *far],
        [shape(4, width)],
    )[0]


def fill_columns(cols, place, blocks, stats):
    for half, sources in enumerate(blocks):
        width = stats.shape[1]
        first = place
        for source in sources:
            size = source.shape[0] * source.shape[1]
            cols[first : first + size, half * width : (half + 1) * width] = standardize(
                flat_rows(source), stats[2 * half : 2 * half + 1], stats[2 * half + 1 : 2 * half + 2]
            )
            first += size
    return first


def inner(left, right):
    return lax.dot_general(
        left, right, (((1,), (1,)), ((), ())), preferred_element_type=f32
    ).astype(bf16)


def gram_kernel(total_rows, ids, *refs):
    mine, one, two, three = refs[:4]
    near, rest, near_whole, far, far_rest, far_whole = refs[4:10]
    pairs = [(near, far)] + [halves(block) for block in refs[10:-4]]
    streams = tuple(zip(*pairs))
    pieces, cols, rows, stats = refs[-4:]
    yl = ids[1]
    width = mine.shape[1]
    own = mine[...] + two[...]
    cross = one[...] + three[...]
    for half in range(2):
        sums = [
            own[2 * half + j : 2 * half + j + 1] + cross[2 - 2 * half + j : 3 - 2 * half + j]
            for j in range(2)
        ]
        mean = sums[0] * (1.0 / total_rows)
        stats[2 * half : 2 * half + 1] = mean
        stats[2 * half + 1 : 2 * half + 2] = lax.rsqrt(
            sums[1] * (1.0 / total_rows) - mean * mean + eps_var
        )
    count = rows.shape[0] // 4
    sources = (
        (near.at[0:2], rest.at[0:2], near_whole.at[0:2], near_whole.at[2:4]),
        (far.at[0:2], far_rest.at[0:2], far_whole.at[2:4], far_whole.at[0:2]),
    )
    for half in range(2):
        for k, source in enumerate(sources[half]):
            place = yl if k % 2 == 0 else 1 - yl
            first = pl.multiple_of((k // 2) * 2 * count + place * count, count)
            rows[pl.ds(first, count), half * width : (half + 1) * width] = standardize(
                flat_rows(source), stats[2 * half : 2 * half + 1], stats[2 * half + 1 : 2 * half + 2]
            )
    last = fill_columns(cols, 0, streams, stats)
    piece = pieces.shape[1]
    for first in range(0, last, piece):
        pieces[first // piece] = inner(cols[first : first + piece], rows[...])


def last_gram_kernel(ids, stats, rows, before, old, left, near, far, *refs):
    parts, (cols, pieces) = refs[:-2], refs[-2:]
    streams = tuple(zip(halves(left), (near, far)))
    del old
    count, piece, _ = before.shape
    x = ids[2]
    fill_columns(cols, count * piece, streams, stats)
    pieces[count ^ x] = inner(cols[count * piece :], rows[...])
    for k in range(count):
        pieces[k ^ x] = before[k]
    for k, part in enumerate(parts):
        part[...] = pieces[k]


def reduce_kernel(ids, *refs):
    total = refs[0][...].astype(f32)
    for ref in refs[1:-2]:
        total = total + ref[...].astype(f32)
    flipped = total.T
    refs[-2][...] = flipped.astype(bf16)
    refs[-1][...] = flipped


def native_kernel(ids, view_a, view_b, mine, theirs, norm, rstd, sums):
    c = ids[0]
    values = []
    for v, view in enumerate((view_a, view_b)):
        stats = jnp.where(c == v, mine[...], theirs[...])
        rstd[v : v + 1] = stats[1:2]
        rounded = standardize(view[...], stats[0:1], stats[1:2])
        norm[v] = rounded
        values.append(rounded.astype(f32))
        sums[v : v + 1] = column_sum(values[v])
    sums[2:3] = column_sum(values[0] * values[1])
    sums[3:4] = jnp.zeros_like(rstd[0:1])


def diagonal(totals, total_rows):
    corr = totals[2:3] * (1.0 / total_rows)
    return corr, -2.0 * (1.0 - corr) - 2.0 * redund_weight * corr


def loss_kernel(total_rows, share, ids, gram, other, totals, loss):
    corr, _ = diagonal(totals[...], total_rows)
    miss = 1.0 - corr
    diag = jnp.sum(miss * miss - redund_weight * (corr * corr), keepdims=True)
    frob = jnp.sum(gram[...] * other[...].astype(f32), keepdims=True)
    weight = 0.5 * redund_weight / (total_rows * total_rows)
    loss[...] = jnp.broadcast_to(share * diag + weight * frob, loss.shape)


def product_kernel(coupling, count_full, ids, *refs):
    full = refs[:count_full]
    cols, rows = refs[count_full : count_full + 2]
    targets, sums = refs[count_full + 2 : -2], refs[-2:]
    x = ids[2]
    piece = full[0].shape[1]
    count, width = targets[0].shape[0] // 2, targets[0].shape[1]
    chunk = width // 2
    lanes = width // 128
    for first_lane in range(0, 2 * width, chunk):
        here = slice(first_lane, first_lane + chunk)
        side, local = divmod(first_lane, width)
        product = None
        for step, part in enumerate(full):
            first = pl.multiple_of((x ^ step) * piece, piece)
            term = jnp.dot(part[...], cols[pl.ds(first, piece), here], preferred_element_type=f32)
            product = term if product is None else product + term
        product = coupling * product
        plain = column_sum(product)
        cross = column_sum(product * rows[:, here].astype(f32))
        for k in range(chunk // 128):
            row = local // 128 + k
            sums[side][row : row + 1] = plain[:, k * 128 : (k + 1) * 128]
            sums[side][lanes + row : lanes + row + 1] = cross[:, k * 128 : (k + 1) * 128]
        for k in range(2):
            target = targets[2 * k + side]
            target[:, local : local + chunk] = product[2 * count * k : 2 * count * (k + 1)].astype(
                target.dtype
            )


def add_kernel(ids, mine, *refs):
    come, (keep, give) = refs[:-2], refs[-2:]
    c = ids[0]
    half = keep.shape[0] // 2
    for h in range(2):
        for out, place in ((keep, c), (give, 1 - c)):
            here = pl.ds(pl.multiple_of((2 * h + place) * half, half), half)
            total = mine[here]
            for ref in come:
                total = total + ref[here].astype(f32)
            out[h * half : (h + 1) * half] = total.astype(out.dtype)


def final_kernel(scale, total_rows, ids, ours, theirs, totals, rstd, norm, mine, other, *outs):
    grad_a, grad_b, loss = outs
    c = ids[0]
    count, width = mine.shape
    lanes = width // 128
    back = [jnp.where(c == v, ours[...], theirs[...]) for v in range(2)]
    loss[...] = back[0][2 * lanes : 2 * lanes + 1] + back[1][2 * lanes : 2 * lanes + 1]
    _, diag_grad = diagonal(totals[...], total_rows)
    diag_grad = diag_grad * (1.0 / total_rows)
    for k in range(lanes):
        here = slice(k * 128, (k + 1) * 128)
        weight = diag_grad[:, here]
        same, cross = mine[:, here], other[:, here].astype(f32)
        for v, out in enumerate((grad_a, grad_b)):
            mean_grad = back[v][k : k + 1] + weight * totals[1 - v : 2 - v, here]
            mean_cross = back[v][lanes + k : lanes + k + 1] + weight * totals[2:3, here]
            grad = jnp.where(c == v, same, cross) + weight * norm[1 - v, :, here].astype(f32)
            out[:, here] = (
                (scale * rstd[v : v + 1, here])
                * (
                    grad
                    - mean_grad * (1.0 / total_rows)
                    - norm[v, :, here].astype(f32) * (mean_cross * (1.0 / total_rows))
                )
            ).astype(bf16)


def shards(view_a, view_b):
    count, width = view_a.shape
    total_rows = count * lax.axis_size(ROWS)
    places = [lax.axis_index(name) for name in ("c", "yl", "x")]
    ids = jnp.stack(places).astype(jnp.int32)
    half = count // 2
    block = shape(2, half, width, dtype=bf16)
    hops = lax.axis_size("z") // 2
    peers = lax.axis_size("x")

    first = places[0] == 0
    keep, give = jnp.where(first, view_a, view_b), jnp.where(first, view_b, view_a)
    near, rest, whole = call(
        split_kernel,
        "split",
        ids,
        [keep, swap(give, "c", 1)],
        [block, block, shape(4, half, width, dtype=bf16)],
    )

    far = swap(rest, RING, 1)
    whole_far, near_far, whole_near = swap(whole, RING, 3), swap(near, RING, 1), swap(whole, RING, 2)
    moments = add_moments(ids, [], [near], [far])
    opposite = shift(moments, hops)
    first = [shift(near, 1), shift(far, 1), shift(near, -1), shift(far, -1)]
    right, left = call(merge_kernel, "merge", ids, first, [shape(4, half, width, dtype=bf16)] * 2)
    right, left = tie((right, left), whole_far)
    moments = add_moments(ids, [moments], first[0::2], first[1::2])
    early, late = [right, left], []
    for hop in range(2, hops):
        if hop == 3:
            right, left = tie((right, left), whole_near, opposite, moments)
        right, left = shift(right, 1), shift(left, -1)
        last = hop == hops - 1
        early, late = early + [right] + [left] * (not last), late + [left] * last
        moments = add_moments(ids, [moments] + [opposite] * last, [right, left], [])
    right, left = tie((right, left), near_far)
    late += [shift(right[:2], 1), shift(left[2:], -1)]
    row_blocks = [near, rest, whole_near, far, near_far, whole_far]
    panel = 2 * half * lax.axis_size("z")
    piece = panel // peers
    pieces, cols, rows, stats = call(
        lambda *refs: gram_kernel(total_rows, *refs),
        "gram",
        ids,
        [moments] + [swap(moments, RING, k) for k in (1, 2, 3)] + row_blocks + early,
        [
            shape(peers - 1, piece, 4 * count, dtype=bf16),
            shape(panel, 2 * width, dtype=bf16),
            shape(4 * count, 2 * width, dtype=bf16),
            shape(4, width),
        ],
        flops=4 * count * panel * width * 3,
    )
    *parts, cols = call(
        last_gram_kernel,
        "last_gram",
        ids,
        [stats, rows, pieces, cols] + late,
        [shape(piece, 4 * count, dtype=bf16)] * peers + [shape(panel, 2 * width, dtype=bf16)],
        [pltpu.VMEM((peers, piece, 4 * count), bf16)],
        {4: peers},
    )

    come = [swap(parts[k], ("c", "x"), peers | k) for k in range(peers)]
    norm, rstd, sums = call(
        native_kernel,
        "native",
        ids,
        [view_a, view_b, stats[:2], swap(stats[:2], "c", 1)],
        [shape(2, count, width, dtype=bf16), shape(2, width), shape(4, width)],
    )
    sums = exchange_sum(sums, "c", (1,))
    sums = exchange_sum(sums, "yh", (1,))
    come[0] = tie(come[0], sums)
    low_gram, gram = call(
        reduce_kernel,
        "reduce",
        ids,
        come,
        [shape(4 * count, piece, dtype=bf16), shape(4 * count, piece)],
    )
    full = [low_gram] + [swap(low_gram, "x", k) for k in range(1, peers)]
    totals = exchange_sum(sums, "z", (1, 2, 4))
    gram_other = swap(low_gram, "c", 1)
    full[1] = tie(full[1], totals, gram_other)
    lanes = width // 128

    leave = shape(2 * count, width, dtype=bf16)
    mine, leave_far, leave_near, leave_both, near_sums, far_sums = call(
        lambda *refs: product_kernel(
            2.0 * redund_weight / (total_rows * total_rows), peers, *refs
        ),
        "products",
        ids,
        full + [cols, rows],
        [shape(2 * count, width), leave, leave, leave] + [shape(2 * lanes, 128)] * 2,
        flops=16 * count * panel * width,
    )
    come_far, come_both = swap(leave_far, RING, 1), swap(leave_both, RING, 3)
    come_near = swap(leave_near, RING, 2)
    loss = call(
        lambda *refs: loss_kernel(total_rows, 1.0 / lax.axis_size(ROWS), *refs),
        "loss",
        ids,
        [gram, gram_other, tie(totals, far_sums)],
        [shape(8, 128)],
        flops=10**11,
    )[0]
    loss = loss + swap(loss, "x", 1) + swap(loss, "x", 2) + swap(loss, "x", 3)
    sums = exchange_sum(jnp.concatenate([near_sums, loss, far_sums, loss]), "z", (1, 2, 4))
    sums = tie(sums, come_far, come_both, come_near)
    near_sums, far_sums = jnp.split(sums, 2)
    back = near_sums + swap(near_sums, RING, 2) + swap(far_sums, RING, 1) + swap(far_sums, RING, 3)
    keep, give = call(
        add_kernel,
        "add",
        ids,
        [mine, come_far, come_both, come_near],
        [shape(count, width), shape(count, width, dtype=bf16)],
    )
    grad_a, grad_b, loss = call(
        lambda *refs: final_kernel(
            total_rows * total_rows / (redund_weight * WIDTH), total_rows, *refs
        ),
        "finish",
        ids,
        [back, swap(back, "c", 1), totals, rstd, norm, keep, swap(give, "c", 1)],
        [shape(count, width, dtype=bf16)] * 2 + [shape(1, 128)],
    )
    return grad_a, grad_b, loss[0, 0]


def solution(mesh):
    fine = Mesh(mesh.devices.reshape(8, 2, 2, 2, 4), ROWS + FEAT)
    return jax.shard_map(
        shards,
        mesh=fine,
        in_specs=(P(ROWS, FEAT), P(ROWS, FEAT)),
        out_specs=(P(ROWS, FEAT), P(ROWS, FEAT), P()),
        check_vma=False,
    )
```

```python
import jax
import jax.numpy as jnp
from jax import lax
from jax.experimental import pallas as pl
from jax.experimental.pallas import tpu as pltpu
from jax.sharding import Mesh, PartitionSpec as P

WIDTH = 8192

redund_weight = 0.0051
eps_var = 1e-05

ROWS = ("z", "yh", "c")
FEAT = ("yl", "x")
RING = ("yh", "yl")
LIMIT = 24 * 1024 * 1024
VMEM = pl.BlockSpec(memory_space=pltpu.VMEM)
SMEM = pl.BlockSpec(memory_space=pltpu.SMEM)
f32 = jnp.float32
bf16 = jnp.bfloat16


def shape(*dims, dtype=f32):
    return jax.ShapeDtypeStruct(dims, dtype)


def call(kernel, name, ids, args, outs, scratch=(), aliases=(), flops=0):
    return pl.pallas_call(
        kernel,
        in_specs=[SMEM] + [VMEM] * len(args),
        out_specs=[VMEM] * len(outs),
        out_shape=outs,
        scratch_shapes=list(scratch),
        input_output_aliases=dict(aliases),
        cost_estimate=pl.CostEstimate(flops=flops, bytes_accessed=0, transcendentals=0),
        compiler_params=pltpu.CompilerParams(vmem_limit_bytes=LIMIT),
        name=name,
    )(ids, *args)


def swap(values, axes, step):
    count = lax.axis_size(axes)
    return lax.ppermute(values, axes, [(k, k ^ step) for k in range(count)])


def shift(values, steps):
    count = lax.axis_size("z")
    return lax.ppermute(values, "z", [(k, (k + steps) % count) for k in range(count)])


def exchange_sum(values, axes, steps):
    for step in steps:
        values = values + swap(values, axes, step)
    return values


def tie(values, *others):
    return lax.optimization_barrier((values, others))[0]


def standardize(values, mean, rstd):
    return ((values.astype(f32) - mean) * rstd).astype(bf16)


def column_sum(values):
    return jnp.sum(values, 0, keepdims=True)


def flat_rows(block):
    return block[...].reshape(-1, block.shape[-1])


def split_kernel(ids, keep, got, near, rest, whole):
    c, yl = ids[0], ids[1]
    half = keep.shape[0] // 2
    for k, place in enumerate((yl, 1 - yl)):
        here = pl.ds(pl.multiple_of(place * half, half), half)
        out = near if k == 0 else rest
        out[c] = keep[here]
        out[1 - c] = got[here]
        whole[2 * k : 2 * k + 2] = out[...]


def merge_kernel(ids, right_near, right_far, left_near, left_far, right, left):
    right[0:2], right[2:4] = right_near[...], right_far[...]
    left[0:2], left[2:4] = left_near[...], left_far[...]


def halves(block):
    return block.at[0:2], block.at[2:4]


def moments_kernel(given, near_count, ids, *refs):
    moments = refs[-1]
    before, blocks = refs[:given], refs[given:-1]
    if near_count == len(blocks):
        pairs = [halves(block) for block in blocks]
    else:
        pairs = list(zip(blocks[:near_count], blocks[near_count:]))
    for half in range(2):
        for j in range(2):
            row = 2 * half + j
            total = None
            for ref in before:
                term = ref[row : row + 1]
                total = term if total is None else total + term
            for pair in pairs:
                floats = flat_rows(pair[half]).astype(f32)
                term = column_sum(floats * floats if j else floats)
                total = term if total is None else total + term
            moments[row : row + 1] = total


def add_moments(ids, before, near, far):
    width = near[0].shape[-1]
    return call(
        lambda *refs: moments_kernel(len(before), len(near), *refs),
        "moments",
        ids,
        [*before, *near, *far],
        [shape(4, width)],
    )[0]


def fill_columns(cols, place, blocks, stats):
    for half, sources in enumerate(blocks):
        width = stats.shape[1]
        first = place
        for source in sources:
            size = source.shape[0] * source.shape[1]
            cols[first : first + size, half * width : (half + 1) * width] = standardize(
                flat_rows(source), stats[2 * half : 2 * half + 1], stats[2 * half + 1 : 2 * half + 2]
            )
            first += size
    return first


def inner(left, right):
    return lax.dot_general(
        left, right, (((1,), (1,)), ((), ())), preferred_element_type=f32
    ).astype(bf16)


def gram_kernel(total_rows, ids, *refs):
    mine, one, two, three = refs[:4]
    near, rest, near_whole, far, far_rest, far_whole = refs[4:10]
    pairs = [(near, far)] + [halves(block) for block in refs[10:-4]]
    streams = tuple(zip(*pairs))
    pieces, cols, rows, stats = refs[-4:]
    yl = ids[1]
    width = mine.shape[1]
    own = mine[...] + two[...]
    cross = one[...] + three[...]
    for half in range(2):
        sums = [
            own[2 * half + j : 2 * half + j + 1] + cross[2 - 2 * half + j : 3 - 2 * half + j]
            for j in range(2)
        ]
        mean = sums[0] * (1.0 / total_rows)
        stats[2 * half : 2 * half + 1] = mean
        stats[2 * half + 1 : 2 * half + 2] = lax.rsqrt(
            sums[1] * (1.0 / total_rows) - mean * mean + eps_var
        )
    count = rows.shape[0] // 4
    sources = (
        (near.at[0:2], rest.at[0:2], near_whole.at[0:2], near_whole.at[2:4]),
        (far.at[0:2], far_rest.at[0:2], far_whole.at[2:4], far_whole.at[0:2]),
    )
    for half in range(2):
        for k, source in enumerate(sources[half]):
            place = yl if k % 2 == 0 else 1 - yl
            first = pl.multiple_of((k // 2) * 2 * count + place * count, count)
            rows[pl.ds(first, count), half * width : (half + 1) * width] = standardize(
                flat_rows(source), stats[2 * half : 2 * half + 1], stats[2 * half + 1 : 2 * half + 2]
            )
    last = fill_columns(cols, 0, streams, stats)
    piece = pieces.shape[1]
    for first in range(0, last, piece):
        pieces[first // piece] = inner(cols[first : first + piece], rows[...])


def last_gram_kernel(ids, stats, rows, before, old, left, near, far, *refs):
    parts, (cols, pieces) = refs[:-2], refs[-2:]
    streams = tuple(zip(halves(left), (near, far)))
    del old
    count, piece, _ = before.shape
    x = ids[2]
    fill_columns(cols, count * piece, streams, stats)
    pieces[count ^ x] = inner(cols[count * piece :], rows[...])
    for k in range(count):
        pieces[k ^ x] = before[k]
    for k, part in enumerate(parts):
        part[...] = pieces[k]


def reduce_kernel(ids, *refs):
    total = refs[0][...].astype(f32)
    for ref in refs[1:-2]:
        total = total + ref[...].astype(f32)
    flipped = total.T
    refs[-2][...] = flipped.astype(bf16)
    refs[-1][...] = flipped


def native_kernel(ids, view_a, view_b, mine, theirs, norm, rstd, sums):
    c = ids[0]
    values = []
    for v, view in enumerate((view_a, view_b)):
        stats = jnp.where(c == v, mine[...], theirs[...])
        rstd[v : v + 1] = stats[1:2]
        rounded = standardize(view[...], stats[0:1], stats[1:2])
        norm[v] = rounded
        values.append(rounded.astype(f32))
        sums[v : v + 1] = column_sum(values[v])
    sums[2:3] = column_sum(values[0] * values[1])
    sums[3:4] = jnp.zeros_like(rstd[0:1])


def diagonal(totals, total_rows):
    corr = totals[2:3] * (1.0 / total_rows)
    return corr, -2.0 * (1.0 - corr) - 2.0 * redund_weight * corr


def loss_kernel(total_rows, share, ids, gram, other, totals, loss):
    corr, _ = diagonal(totals[...], total_rows)
    miss = 1.0 - corr
    diag = jnp.sum(miss * miss - redund_weight * (corr * corr), keepdims=True)
    frob = jnp.sum(gram[...] * other[...].astype(f32), keepdims=True)
    weight = 0.5 * redund_weight / (total_rows * total_rows)
    loss[...] = jnp.broadcast_to(share * diag + weight * frob, loss.shape)


def product_kernel(coupling, count_full, ids, *refs):
    full = refs[:count_full]
    cols, rows = refs[count_full : count_full + 2]
    targets, sums = refs[count_full + 2 : -2], refs[-2:]
    x = ids[2]
    piece = full[0].shape[1]
    count, width = targets[0].shape[0] // 2, targets[0].shape[1]
    chunk = width // 2
    lanes = width // 128
    for first_lane in range(0, 2 * width, chunk):
        here = slice(first_lane, first_lane + chunk)
        side, local = divmod(first_lane, width)
        product = None
        for step, part in enumerate(full):
            first = pl.multiple_of((x ^ step) * piece, piece)
            term = jnp.dot(part[...], cols[pl.ds(first, piece), here], preferred_element_type=f32)
            product = term if product is None else product + term
        product = coupling * product
        plain = column_sum(product)
        cross = column_sum(product * rows[:, here].astype(f32))
        for k in range(chunk // 128):
            row = local // 128 + k
            sums[side][row : row + 1] = plain[:, k * 128 : (k + 1) * 128]
            sums[side][lanes + row : lanes + row + 1] = cross[:, k * 128 : (k + 1) * 128]
        for k in range(2):
            target = targets[2 * k + side]
            target[:, local : local + chunk] = product[2 * count * k : 2 * count * (k + 1)].astype(
                target.dtype
            )


def add_kernel(ids, mine, *refs):
    come, (keep, give) = refs[:-2], refs[-2:]
    c = ids[0]
    half = keep.shape[0] // 2
    for h in range(2):
        for out, place in ((keep, c), (give, 1 - c)):
            here = pl.ds(pl.multiple_of((2 * h + place) * half, half), half)
            total = mine[here]
            for ref in come:
                total = total + ref[here].astype(f32)
            out[h * half : (h + 1) * half] = total.astype(out.dtype)


def final_kernel(scale, total_rows, ids, ours, theirs, totals, rstd, norm, mine, other, *outs):
    grad_a, grad_b, loss = outs
    c = ids[0]
    count, width = mine.shape
    lanes = width // 128
    back = [jnp.where(c == v, ours[...], theirs[...]) for v in range(2)]
    loss[...] = back[0][2 * lanes : 2 * lanes + 1] + back[1][2 * lanes : 2 * lanes + 1]
    _, diag_grad = diagonal(totals[...], total_rows)
    diag_grad = diag_grad * (1.0 / total_rows)
    for k in range(lanes):
        here = slice(k * 128, (k + 1) * 128)
        weight = diag_grad[:, here]
        same, cross = mine[:, here], other[:, here].astype(f32)
        for v, out in enumerate((grad_a, grad_b)):
            mean_grad = back[v][k : k + 1] + weight * totals[1 - v : 2 - v, here]
            mean_cross = back[v][lanes + k : lanes + k + 1] + weight * totals[2:3, here]
            grad = jnp.where(c == v, same, cross) + weight * norm[1 - v, :, here].astype(f32)
            out[:, here] = (
                (scale * rstd[v : v + 1, here])
                * (
                    grad
                    - mean_grad * (1.0 / total_rows)
                    - norm[v, :, here].astype(f32) * (mean_cross * (1.0 / total_rows))
                )
            ).astype(bf16)


def shards(view_a, view_b):
    count, width = view_a.shape
    total_rows = count * lax.axis_size(ROWS)
    places = [lax.axis_index(name) for name in ("c", "yl", "x")]
    ids = jnp.stack(places).astype(jnp.int32)
    half = count // 2
    block = shape(2, half, width, dtype=bf16)
    hops = lax.axis_size("z") // 2
    peers = lax.axis_size("x")

    first = places[0] == 0
    keep, give = jnp.where(first, view_a, view_b), jnp.where(first, view_b, view_a)
    near, rest, whole = call(
        split_kernel,
        "split",
        ids,
        [keep, swap(give, "c", 1)],
        [block, block, shape(4, half, width, dtype=bf16)],
    )

    far = swap(rest, RING, 1)
    whole_far, near_far, whole_near = swap(whole, RING, 3), swap(near, RING, 1), swap(whole, RING, 2)
    moments = add_moments(ids, [], [near], [far])
    opposite = shift(moments, hops)
    first = [shift(near, 1), shift(far, 1), shift(near, -1), shift(far, -1)]
    right, left = call(merge_kernel, "merge", ids, first, [shape(4, half, width, dtype=bf16)] * 2)
    right, left = tie((right, left), whole_far)
    moments = add_moments(ids, [moments], first[0::2], first[1::2])
    early, late = [right, left], []
    for hop in range(2, hops):
        if hop == 3:
            right, left = tie((right, left), whole_near, opposite, moments)
        right, left = shift(right, 1), shift(left, -1)
        last = hop == hops - 1
        early, late = early + [right] + [left] * (not last), late + [left] * last
        moments = add_moments(ids, [moments] + [opposite] * last, [right, left], [])
    right, left = tie((right, left), near_far)
    late += [shift(right[:2], 1), shift(left[2:], -1)]
    row_blocks = [near, rest, whole_near, far, near_far, whole_far]
    panel = 2 * half * lax.axis_size("z")
    piece = panel // peers
    pieces, cols, rows, stats = call(
        lambda *refs: gram_kernel(total_rows, *refs),
        "gram",
        ids,
        [moments] + [swap(moments, RING, k) for k in (1, 2, 3)] + row_blocks + early,
        [
            shape(peers - 1, piece, 4 * count, dtype=bf16),
            shape(panel, 2 * width, dtype=bf16),
            shape(4 * count, 2 * width, dtype=bf16),
            shape(4, width),
        ],
        flops=4 * count * panel * width * 3,
    )
    *parts, cols = call(
        last_gram_kernel,
        "last_gram",
        ids,
        [stats, rows, pieces, cols] + late,
        [shape(piece, 4 * count, dtype=bf16)] * peers + [shape(panel, 2 * width, dtype=bf16)],
        [pltpu.VMEM((peers, piece, 4 * count), bf16)],
        {4: peers},
    )

    come = [swap(parts[k], ("c", "x"), peers | k) for k in range(peers)]
    norm, rstd, sums = call(
        native_kernel,
        "native",
        ids,
        [view_a, view_b, stats[:2], swap(stats[:2], "c", 1)],
        [shape(2, count, width, dtype=bf16), shape(2, width), shape(4, width)],
    )
    sums = exchange_sum(sums, "c", (1,))
    sums = exchange_sum(sums, "yh", (1,))
    sums = exchange_sum(sums, "z", (1,))
    come[0] = tie(come[0], sums)
    low_gram, gram = call(
        reduce_kernel,
        "reduce",
        ids,
        come,
        [shape(4 * count, piece, dtype=bf16), shape(4 * count, piece)],
    )
    full = [low_gram] + [swap(low_gram, "x", k) for k in range(1, peers)]
    totals = exchange_sum(sums, "z", (2, 4))
    gram_other = swap(low_gram, "c", 1)
    full[1] = tie(full[1], totals, gram_other)
    lanes = width // 128

    leave = shape(2 * count, width, dtype=bf16)
    mine, leave_far, leave_near, leave_both, near_sums, far_sums = call(
        lambda *refs: product_kernel(
            2.0 * redund_weight / (total_rows * total_rows), peers, *refs
        ),
        "products",
        ids,
        full + [cols, rows],
        [shape(2 * count, width), leave, leave, leave] + [shape(2 * lanes, 128)] * 2,
        flops=16 * count * panel * width,
    )
    come_far, come_both = swap(leave_far, RING, 1), swap(leave_both, RING, 3)
    come_near = swap(leave_near, RING, 2)
    loss = call(
        lambda *refs: loss_kernel(total_rows, 1.0 / lax.axis_size(ROWS), *refs),
        "loss",
        ids,
        [gram, gram_other, tie(totals, far_sums)],
        [shape(8, 128)],
        flops=10**11,
    )[0]
    loss = loss + swap(loss, "x", 1) + swap(loss, "x", 2) + swap(loss, "x", 3)
    sums = exchange_sum(jnp.concatenate([near_sums, loss, far_sums, loss]), "z", (1, 2, 4))
    sums = tie(sums, come_far, come_both, come_near)
    near_sums, far_sums = jnp.split(sums, 2)
    back = near_sums + swap(near_sums, RING, 2) + swap(far_sums, RING, 1) + swap(far_sums, RING, 3)
    keep, give = call(
        add_kernel,
        "add",
        ids,
        [mine, come_far, come_both, come_near],
        [shape(count, width), shape(count, width, dtype=bf16)],
    )
    grad_a, grad_b, loss = call(
        lambda *refs: final_kernel(
            total_rows * total_rows / (redund_weight * WIDTH), total_rows, *refs
        ),
        "finish",
        ids,
        [back, swap(back, "c", 1), totals, rstd, norm, keep, swap(give, "c", 1)],
        [shape(count, width, dtype=bf16)] * 2 + [shape(1, 128)],
    )
    return grad_a, grad_b, loss[0, 0]


def solution(mesh):
    fine = Mesh(mesh.devices.reshape(8, 2, 2, 2, 4), ROWS + FEAT)
    return jax.shard_map(
        shards,
        mesh=fine,
        in_specs=(P(ROWS, FEAT), P(ROWS, FEAT)),
        out_specs=(P(ROWS, FEAT), P(ROWS, FEAT), P()),
        check_vma=False,
    )
```

```python
import jax
import jax.numpy as jnp
from jax import lax
from jax.experimental import pallas as pl
from jax.experimental.pallas import tpu as pltpu
from jax.sharding import Mesh, PartitionSpec as P

WIDTH = 8192

redund_weight = 0.0051
eps_var = 1e-05

ROWS = ("z", "yh", "c")
FEAT = ("yl", "x")
RING = ("yh", "yl")
LIMIT = 24 * 1024 * 1024
VMEM = pl.BlockSpec(memory_space=pltpu.VMEM)
SMEM = pl.BlockSpec(memory_space=pltpu.SMEM)
f32 = jnp.float32
bf16 = jnp.bfloat16


def shape(*dims, dtype=f32):
    return jax.ShapeDtypeStruct(dims, dtype)


def call(kernel, name, ids, args, outs, scratch=(), aliases=(), flops=0):
    return pl.pallas_call(
        kernel,
        in_specs=[SMEM] + [VMEM] * len(args),
        out_specs=[VMEM] * len(outs),
        out_shape=outs,
        scratch_shapes=list(scratch),
        input_output_aliases=dict(aliases),
        cost_estimate=pl.CostEstimate(flops=flops, bytes_accessed=0, transcendentals=0),
        compiler_params=pltpu.CompilerParams(vmem_limit_bytes=LIMIT),
        name=name,
    )(ids, *args)


def swap(values, axes, step):
    count = lax.axis_size(axes)
    return lax.ppermute(values, axes, [(k, k ^ step) for k in range(count)])


def shift(values, steps):
    count = lax.axis_size("z")
    return lax.ppermute(values, "z", [(k, (k + steps) % count) for k in range(count)])


def exchange_sum(values, axes, steps):
    for step in steps:
        values = values + swap(values, axes, step)
    return values


def tie(values, *others):
    return lax.optimization_barrier((values, others))[0]


def standardize(values, mean, rstd):
    return ((values.astype(f32) - mean) * rstd).astype(bf16)


def column_sum(values):
    return jnp.sum(values, 0, keepdims=True)


def flat_rows(block):
    return block[...].reshape(-1, block.shape[-1])


def split_kernel(ids, keep, got, near, rest, whole):
    c, yl = ids[0], ids[1]
    half = keep.shape[0] // 2
    for k, place in enumerate((yl, 1 - yl)):
        here = pl.ds(pl.multiple_of(place * half, half), half)
        out = near if k == 0 else rest
        out[c] = keep[here]
        out[1 - c] = got[here]
        whole[2 * k : 2 * k + 2] = out[...]


def merge_kernel(ids, right_near, right_far, left_near, left_far, right, left):
    right[0:2], right[2:4] = right_near[...], right_far[...]
    left[0:2], left[2:4] = left_near[...], left_far[...]


def halves(block):
    return block.at[0:2], block.at[2:4]


def moments_kernel(given, near_count, ids, *refs):
    moments = refs[-1]
    before, blocks = refs[:given], refs[given:-1]
    if near_count == len(blocks):
        pairs = [halves(block) for block in blocks]
    else:
        pairs = list(zip(blocks[:near_count], blocks[near_count:]))
    for half in range(2):
        for j in range(2):
            row = 2 * half + j
            total = None
            for ref in before:
                term = ref[row : row + 1]
                total = term if total is None else total + term
            for pair in pairs:
                floats = flat_rows(pair[half]).astype(f32)
                term = column_sum(floats * floats if j else floats)
                total = term if total is None else total + term
            moments[row : row + 1] = total


def add_moments(ids, before, near, far):
    width = near[0].shape[-1]
    return call(
        lambda *refs: moments_kernel(len(before), len(near), *refs),
        "moments",
        ids,
        [*before, *near, *far],
        [shape(4, width)],
    )[0]


def fill_columns(cols, place, blocks, stats):
    for half, sources in enumerate(blocks):
        width = stats.shape[1]
        first = place
        for source in sources:
            size = source.shape[0] * source.shape[1]
            cols[first : first + size, half * width : (half + 1) * width] = standardize(
                flat_rows(source), stats[2 * half : 2 * half + 1], stats[2 * half + 1 : 2 * half + 2]
            )
            first += size
    return first


def inner(left, right):
    return lax.dot_general(
        left, right, (((1,), (1,)), ((), ())), preferred_element_type=f32
    ).astype(bf16)


def gram_kernel(total_rows, ids, *refs):
    mine, one, two, three = refs[:4]
    near, rest, near_whole, far, far_rest, far_whole = refs[4:10]
    pairs = [(near, far)] + [halves(block) for block in refs[10:-4]]
    streams = tuple(zip(*pairs))
    pieces, cols, rows, stats = refs[-4:]
    yl = ids[1]
    width = mine.shape[1]
    own = mine[...] + two[...]
    cross = one[...] + three[...]
    for half in range(2):
        sums = [
            own[2 * half + j : 2 * half + j + 1] + cross[2 - 2 * half + j : 3 - 2 * half + j]
            for j in range(2)
        ]
        mean = sums[0] * (1.0 / total_rows)
        stats[2 * half : 2 * half + 1] = mean
        stats[2 * half + 1 : 2 * half + 2] = lax.rsqrt(
            sums[1] * (1.0 / total_rows) - mean * mean + eps_var
        )
    count = rows.shape[0] // 4
    sources = (
        (near.at[0:2], rest.at[0:2], near_whole.at[0:2], near_whole.at[2:4]),
        (far.at[0:2], far_rest.at[0:2], far_whole.at[2:4], far_whole.at[0:2]),
    )
    for half in range(2):
        for k, source in enumerate(sources[half]):
            place = yl if k % 2 == 0 else 1 - yl
            first = pl.multiple_of((k // 2) * 2 * count + place * count, count)
            rows[pl.ds(first, count), half * width : (half + 1) * width] = standardize(
                flat_rows(source), stats[2 * half : 2 * half + 1], stats[2 * half + 1 : 2 * half + 2]
            )
    last = fill_columns(cols, 0, streams, stats)
    piece = pieces.shape[1]
    for first in range(0, last, piece):
        pieces[first // piece] = inner(cols[first : first + piece], rows[...])


def last_gram_kernel(ids, stats, rows, before, old, left, near, far, *refs):
    parts, (cols, pieces) = refs[:-2], refs[-2:]
    streams = tuple(zip(halves(left), (near, far)))
    del old
    count, piece, _ = before.shape
    x = ids[2]
    fill_columns(cols, count * piece, streams, stats)
    pieces[count ^ x] = inner(cols[count * piece :], rows[...])
    for k in range(count):
        pieces[k ^ x] = before[k]
    for k, part in enumerate(parts):
        part[...] = pieces[k]


def reduce_kernel(ids, *refs):
    total = refs[0][...].astype(f32)
    for ref in refs[1:-2]:
        total = total + ref[...].astype(f32)
    flipped = total.T
    refs[-2][...] = flipped.astype(bf16)
    refs[-1][...] = flipped


def native_kernel(ids, view_a, view_b, mine, theirs, norm, rstd, sums):
    c = ids[0]
    values = []
    for v, view in enumerate((view_a, view_b)):
        stats = jnp.where(c == v, mine[...], theirs[...])
        rstd[v : v + 1] = stats[1:2]
        rounded = standardize(view[...], stats[0:1], stats[1:2])
        norm[v] = rounded
        values.append(rounded.astype(f32))
        sums[v : v + 1] = column_sum(values[v])
    sums[2:3] = column_sum(values[0] * values[1])
    sums[3:4] = jnp.zeros_like(rstd[0:1])


def diagonal(totals, total_rows):
    corr = totals[2:3] * (1.0 / total_rows)
    return corr, -2.0 * (1.0 - corr) - 2.0 * redund_weight * corr


def loss_kernel(total_rows, share, ids, gram, other, totals, loss):
    corr, _ = diagonal(totals[...], total_rows)
    miss = 1.0 - corr
    diag = jnp.sum(miss * miss - redund_weight * (corr * corr), keepdims=True)
    frob = jnp.sum(gram[...] * other[...].astype(f32), keepdims=True)
    weight = 0.5 * redund_weight / (total_rows * total_rows)
    loss[...] = jnp.broadcast_to(share * diag + weight * frob, loss.shape)


def product_kernel(coupling, side, count_full, ids, *refs):
    full = refs[:count_full]
    cols, rows = refs[count_full : count_full + 2]
    targets, sums = refs[count_full + 2 : -1], refs[-1]
    x = ids[2]
    piece = full[0].shape[1]
    count, width = targets[0].shape[0] // 2, targets[0].shape[1]
    chunk = width // 2
    lanes = width // 128
    for local in range(0, width, chunk):
        here = slice(side * width + local, side * width + local + chunk)
        product = None
        for step, part in enumerate(full):
            first = pl.multiple_of((x ^ step) * piece, piece)
            term = jnp.dot(part[...], cols[pl.ds(first, piece), here], preferred_element_type=f32)
            product = term if product is None else product + term
        product = coupling * product
        plain = column_sum(product)
        cross = column_sum(product * rows[:, here].astype(f32))
        for k in range(chunk // 128):
            row = local // 128 + k
            sums[row : row + 1] = plain[:, k * 128 : (k + 1) * 128]
            sums[lanes + row : lanes + row + 1] = cross[:, k * 128 : (k + 1) * 128]
        for k, target in enumerate(targets):
            target[:, local : local + chunk] = product[2 * count * k : 2 * count * (k + 1)].astype(
                target.dtype
            )


def add_kernel(ids, mine, *refs):
    come, (keep, give) = refs[:-2], refs[-2:]
    c = ids[0]
    half = keep.shape[0] // 2
    for h in range(2):
        for out, place in ((keep, c), (give, 1 - c)):
            here = pl.ds(pl.multiple_of((2 * h + place) * half, half), half)
            total = mine[here]
            for ref in come:
                total = total + ref[here].astype(f32)
            out[h * half : (h + 1) * half] = total.astype(out.dtype)


def final_kernel(scale, total_rows, ids, ours, theirs, totals, rstd, norm, mine, other, *outs):
    grad_a, grad_b, loss = outs
    c = ids[0]
    count, width = mine.shape
    lanes = width // 128
    back = [jnp.where(c == v, ours[...], theirs[...]) for v in range(2)]
    loss[...] = back[0][2 * lanes : 2 * lanes + 1] + back[1][2 * lanes : 2 * lanes + 1]
    _, diag_grad = diagonal(totals[...], total_rows)
    diag_grad = diag_grad * (1.0 / total_rows)
    for k in range(lanes):
        here = slice(k * 128, (k + 1) * 128)
        weight = diag_grad[:, here]
        same, cross = mine[:, here], other[:, here].astype(f32)
        for v, out in enumerate((grad_a, grad_b)):
            mean_grad = back[v][k : k + 1] + weight * totals[1 - v : 2 - v, here]
            mean_cross = back[v][lanes + k : lanes + k + 1] + weight * totals[2:3, here]
            grad = jnp.where(c == v, same, cross) + weight * norm[1 - v, :, here].astype(f32)
            out[:, here] = (
                (scale * rstd[v : v + 1, here])
                * (
                    grad
                    - mean_grad * (1.0 / total_rows)
                    - norm[v, :, here].astype(f32) * (mean_cross * (1.0 / total_rows))
                )
            ).astype(bf16)


def shards(view_a, view_b):
    count, width = view_a.shape
    total_rows = count * lax.axis_size(ROWS)
    places = [lax.axis_index(name) for name in ("c", "yl", "x")]
    ids = jnp.stack(places).astype(jnp.int32)
    half = count // 2
    block = shape(2, half, width, dtype=bf16)
    hops = lax.axis_size("z") // 2
    peers = lax.axis_size("x")

    first = places[0] == 0
    keep, give = jnp.where(first, view_a, view_b), jnp.where(first, view_b, view_a)
    near, rest, whole = call(
        split_kernel,
        "split",
        ids,
        [keep, swap(give, "c", 1)],
        [block, block, shape(4, half, width, dtype=bf16)],
    )

    far = swap(rest, RING, 1)
    whole_far, near_far, whole_near = swap(whole, RING, 3), swap(near, RING, 1), swap(whole, RING, 2)
    moments = add_moments(ids, [], [near], [far])
    opposite = shift(moments, hops)
    first = [shift(near, 1), shift(far, 1), shift(near, -1), shift(far, -1)]
    right, left = call(merge_kernel, "merge", ids, first, [shape(4, half, width, dtype=bf16)] * 2)
    right, left = tie((right, left), whole_far)
    moments = add_moments(ids, [moments], first[0::2], first[1::2])
    early, late = [right, left], []
    for hop in range(2, hops):
        if hop == 3:
            right, left = tie((right, left), whole_near, opposite, moments)
        right, left = shift(right, 1), shift(left, -1)
        last = hop == hops - 1
        early, late = early + [right] + [left] * (not last), late + [left] * last
        moments = add_moments(ids, [moments] + [opposite] * last, [right, left], [])
    right, left = tie((right, left), near_far)
    late += [shift(right[:2], 1), shift(left[2:], -1)]
    row_blocks = [near, rest, whole_near, far, near_far, whole_far]
    panel = 2 * half * lax.axis_size("z")
    piece = panel // peers
    pieces, cols, rows, stats = call(
        lambda *refs: gram_kernel(total_rows, *refs),
        "gram",
        ids,
        [moments] + [swap(moments, RING, k) for k in (1, 2, 3)] + row_blocks + early,
        [
            shape(peers - 1, piece, 4 * count, dtype=bf16),
            shape(panel, 2 * width, dtype=bf16),
            shape(4 * count, 2 * width, dtype=bf16),
            shape(4, width),
        ],
        flops=4 * count * panel * width * 3,
    )
    *parts, cols = call(
        last_gram_kernel,
        "last_gram",
        ids,
        [stats, rows, pieces, cols] + late,
        [shape(piece, 4 * count, dtype=bf16)] * peers + [shape(panel, 2 * width, dtype=bf16)],
        [pltpu.VMEM((peers, piece, 4 * count), bf16)],
        {4: peers},
    )

    come = [swap(parts[k], ("c", "x"), peers | k) for k in range(peers)]
    norm, rstd, sums = call(
        native_kernel,
        "native",
        ids,
        [view_a, view_b, stats[:2], swap(stats[:2], "c", 1)],
        [shape(2, count, width, dtype=bf16), shape(2, width), shape(4, width)],
    )
    sums = exchange_sum(sums, "c", (1,))
    sums = exchange_sum(sums, "yh", (1,))
    sums = exchange_sum(sums, "z", (1,))
    come[0] = tie(come[0], sums)
    low_gram, gram = call(
        reduce_kernel,
        "reduce",
        ids,
        come,
        [shape(4 * count, piece, dtype=bf16), shape(4 * count, piece)],
    )
    full = [low_gram] + [swap(low_gram, "x", k) for k in range(1, peers)]
    totals = exchange_sum(sums, "z", (2, 4))
    gram_other = swap(low_gram, "c", 1)
    full[1] = tie(full[1], totals, gram_other)
    lanes = width // 128


    def product(side, dtype, flops):
        return call(
            lambda *refs: product_kernel(
                2.0 * redund_weight / (total_rows * total_rows), side, peers, *refs
            ),
            "products",
            ids,
            full + [cols, rows],
            [shape(2 * count, width, dtype=dtype), shape(2 * count, width, dtype=bf16)]
            + [shape(2 * lanes, 128)],
            flops=flops,
        )

    leave_far, leave_both, far_sums = product(1, bf16, 8 * count * panel * width)
    mine, leave_near, near_sums = product(0, f32, 10**11)
    come_far, come_both = swap(leave_far, RING, 1), swap(leave_both, RING, 3)
    come_near = swap(leave_near, RING, 2)
    loss = call(
        lambda *refs: loss_kernel(total_rows, 1.0 / lax.axis_size(ROWS), *refs),
        "loss",
        ids,
        [gram, gram_other, tie(totals, far_sums)],
        [shape(8, 128)],
        flops=10**11,
    )[0]
    loss = loss + swap(loss, "x", 1) + swap(loss, "x", 2) + swap(loss, "x", 3)
    sums = exchange_sum(jnp.concatenate([near_sums, loss, far_sums, loss]), "z", (1, 2, 4))
    sums = tie(sums, come_far, come_both, come_near)
    near_sums, far_sums = jnp.split(sums, 2)
    back = near_sums + swap(near_sums, RING, 2) + swap(far_sums, RING, 1) + swap(far_sums, RING, 3)
    keep, give = call(
        add_kernel,
        "add",
        ids,
        [mine, come_far, come_both, come_near],
        [shape(count, width), shape(count, width, dtype=bf16)],
    )
    grad_a, grad_b, loss = call(
        lambda *refs: final_kernel(
            total_rows * total_rows / (redund_weight * WIDTH), total_rows, *refs
        ),
        "finish",
        ids,
        [back, swap(back, "c", 1), totals, rstd, norm, keep, swap(give, "c", 1)],
        [shape(count, width, dtype=bf16)] * 2 + [shape(1, 128)],
    )
    return grad_a, grad_b, loss[0, 0]


def solution(mesh):
    fine = Mesh(mesh.devices.reshape(8, 2, 2, 2, 4), ROWS + FEAT)
    return jax.shard_map(
        shards,
        mesh=fine,
        in_specs=(P(ROWS, FEAT), P(ROWS, FEAT)),
        out_specs=(P(ROWS, FEAT), P(ROWS, FEAT), P()),
        check_vma=False,
    )
```

```python
import jax
import jax.numpy as jnp
from jax import lax
from jax.experimental import pallas as pl
from jax.experimental.pallas import tpu as pltpu
from jax.sharding import Mesh, PartitionSpec as P

WIDTH = 8192

redund_weight = 0.0051
eps_var = 1e-05

ROWS = ("z", "yh", "c")
FEAT = ("yl", "x")
RING = ("yh", "yl")
LIMIT = 24 * 1024 * 1024
VMEM = pl.BlockSpec(memory_space=pltpu.VMEM)
SMEM = pl.BlockSpec(memory_space=pltpu.SMEM)
f32 = jnp.float32
bf16 = jnp.bfloat16


def shape(*dims, dtype=f32):
    return jax.ShapeDtypeStruct(dims, dtype)


def call(kernel, name, ids, args, outs, scratch=(), aliases=(), flops=0):
    return pl.pallas_call(
        kernel,
        in_specs=[SMEM] + [VMEM] * len(args),
        out_specs=[VMEM] * len(outs),
        out_shape=outs,
        scratch_shapes=list(scratch),
        input_output_aliases=dict(aliases),
        cost_estimate=pl.CostEstimate(flops=flops, bytes_accessed=0, transcendentals=0),
        compiler_params=pltpu.CompilerParams(vmem_limit_bytes=LIMIT),
        name=name,
    )(ids, *args)


def swap(values, axes, step):
    count = lax.axis_size(axes)
    return lax.ppermute(values, axes, [(k, k ^ step) for k in range(count)])


def shift(values, steps):
    count = lax.axis_size("z")
    return lax.ppermute(values, "z", [(k, (k + steps) % count) for k in range(count)])


def exchange_sum(values, axes, steps):
    for step in steps:
        values = values + swap(values, axes, step)
    return values


def tie(values, *others):
    return lax.optimization_barrier((values, others))[0]


def standardize(values, mean, rstd):
    return ((values.astype(f32) - mean) * rstd).astype(bf16)


def column_sum(values):
    return jnp.sum(values, 0, keepdims=True)


def flat_rows(block):
    return block[...].reshape(-1, block.shape[-1])


def split_kernel(ids, keep, got, near, rest, whole):
    c, yl = ids[0], ids[1]
    half = keep.shape[0] // 2
    for k, place in enumerate((yl, 1 - yl)):
        here = pl.ds(pl.multiple_of(place * half, half), half)
        out = near if k == 0 else rest
        out[c] = keep[here]
        out[1 - c] = got[here]
        whole[2 * k : 2 * k + 2] = out[...]


def merge_kernel(ids, right_near, right_far, left_near, left_far, right, left):
    right[0:2], right[2:4] = right_near[...], right_far[...]
    left[0:2], left[2:4] = left_near[...], left_far[...]


def halves(block):
    return block.at[0:2], block.at[2:4]


def moments_kernel(given, near_count, ids, *refs):
    moments = refs[-1]
    before, blocks = refs[:given], refs[given:-1]
    if near_count == len(blocks):
        pairs = [halves(block) for block in blocks]
    else:
        pairs = list(zip(blocks[:near_count], blocks[near_count:]))
    for half in range(2):
        for j in range(2):
            row = 2 * half + j
            total = None
            for ref in before:
                term = ref[row : row + 1]
                total = term if total is None else total + term
            for pair in pairs:
                floats = flat_rows(pair[half]).astype(f32)
                term = column_sum(floats * floats if j else floats)
                total = term if total is None else total + term
            moments[row : row + 1] = total


def add_moments(ids, before, near, far):
    width = near[0].shape[-1]
    return call(
        lambda *refs: moments_kernel(len(before), len(near), *refs),
        "moments",
        ids,
        [*before, *near, *far],
        [shape(4, width)],
    )[0]


def fill_columns(cols, place, blocks, stats):
    for half, sources in enumerate(blocks):
        width = stats.shape[1]
        first = place
        for source in sources:
            size = source.shape[0] * source.shape[1]
            cols[first : first + size, half * width : (half + 1) * width] = standardize(
                flat_rows(source), stats[2 * half : 2 * half + 1], stats[2 * half + 1 : 2 * half + 2]
            )
            first += size
    return first


def inner(left, right):
    return lax.dot_general(
        left, right, (((1,), (1,)), ((), ())), preferred_element_type=f32
    ).astype(bf16)


def gram_kernel(total_rows, ids, *refs):
    mine, one, two, three = refs[:4]
    near, rest, near_whole, far, far_rest, far_whole = refs[4:10]
    pairs = [(near, far)] + [halves(block) for block in refs[10:-4]]
    streams = tuple(zip(*pairs))
    pieces, cols, rows, stats = refs[-4:]
    yl = ids[1]
    width = mine.shape[1]
    own = mine[...] + two[...]
    cross = one[...] + three[...]
    for half in range(2):
        sums = [
            own[2 * half + j : 2 * half + j + 1] + cross[2 - 2 * half + j : 3 - 2 * half + j]
            for j in range(2)
        ]
        mean = sums[0] * (1.0 / total_rows)
        stats[2 * half : 2 * half + 1] = mean
        stats[2 * half + 1 : 2 * half + 2] = lax.rsqrt(
            sums[1] * (1.0 / total_rows) - mean * mean + eps_var
        )
    count = rows.shape[0] // 4
    sources = (
        (near.at[0:2], rest.at[0:2], near_whole.at[0:2], near_whole.at[2:4]),
        (far.at[0:2], far_rest.at[0:2], far_whole.at[2:4], far_whole.at[0:2]),
    )
    for half in range(2):
        for k, source in enumerate(sources[half]):
            place = yl if k % 2 == 0 else 1 - yl
            first = pl.multiple_of((k // 2) * 2 * count + place * count, count)
            rows[pl.ds(first, count), half * width : (half + 1) * width] = standardize(
                flat_rows(source), stats[2 * half : 2 * half + 1], stats[2 * half + 1 : 2 * half + 2]
            )
    last = fill_columns(cols, 0, streams, stats)
    piece = pieces.shape[1]
    for first in range(0, last, piece):
        pieces[first // piece] = inner(cols[first : first + piece], rows[...])


def last_gram_kernel(ids, stats, rows, before, old, left, near, far, *refs):
    parts, (cols, pieces) = refs[:-2], refs[-2:]
    streams = tuple(zip(halves(left), (near, far)))
    del old
    count, piece, _ = before.shape
    x = ids[2]
    fill_columns(cols, count * piece, streams, stats)
    pieces[count ^ x] = inner(cols[count * piece :], rows[...])
    for k in range(count):
        pieces[k ^ x] = before[k]
    for k, part in enumerate(parts):
        part[...] = pieces[k]


def reduce_kernel(ids, *refs):
    total = refs[0][...].astype(f32)
    for ref in refs[1:-2]:
        total = total + ref[...].astype(f32)
    flipped = total.T
    refs[-2][...] = flipped.astype(bf16)
    refs[-1][...] = flipped


def native_kernel(ids, view_a, view_b, mine, theirs, norm, rstd, sums):
    c = ids[0]
    values = []
    for v, view in enumerate((view_a, view_b)):
        stats = jnp.where(c == v, mine[...], theirs[...])
        rstd[v : v + 1] = stats[1:2]
        rounded = standardize(view[...], stats[0:1], stats[1:2])
        norm[v] = rounded
        values.append(rounded.astype(f32))
        sums[v : v + 1] = column_sum(values[v])
    sums[2:3] = column_sum(values[0] * values[1])
    sums[3:4] = jnp.zeros_like(rstd[0:1])


def diagonal(totals, total_rows):
    corr = totals[2:3] * (1.0 / total_rows)
    return corr, -2.0 * (1.0 - corr) - 2.0 * redund_weight * corr


def loss_kernel(total_rows, share, ids, gram, other, totals, loss):
    corr, _ = diagonal(totals[...], total_rows)
    miss = 1.0 - corr
    diag = jnp.sum(miss * miss - redund_weight * (corr * corr), keepdims=True)
    frob = jnp.sum(gram[...] * other[...].astype(f32), keepdims=True)
    weight = 0.5 * redund_weight / (total_rows * total_rows)
    loss[...] = jnp.broadcast_to(share * diag + weight * frob, loss.shape)


def product_kernel(coupling, side, count_full, ids, *refs):
    full = refs[:count_full]
    cols, rows = refs[count_full : count_full + 2]
    targets, sums = refs[count_full + 2 : -1], refs[-1]
    x = ids[2]
    piece = full[0].shape[1]
    count, width = targets[0].shape[0] // 2, targets[0].shape[1]
    chunk = width // 2
    lanes = width // 128
    for local in range(0, width, chunk):
        here = slice(side * width + local, side * width + local + chunk)
        product = None
        for step, part in enumerate(full):
            first = pl.multiple_of((x ^ step) * piece, piece)
            term = jnp.dot(part[...], cols[pl.ds(first, piece), here], preferred_element_type=f32)
            product = term if product is None else product + term
        product = coupling * product
        plain = column_sum(product)
        cross = column_sum(product * rows[:, here].astype(f32))
        for k in range(chunk // 128):
            row = local // 128 + k
            sums[row : row + 1] = plain[:, k * 128 : (k + 1) * 128]
            sums[lanes + row : lanes + row + 1] = cross[:, k * 128 : (k + 1) * 128]
        for k, target in enumerate(targets):
            target[:, local : local + chunk] = product[2 * count * k : 2 * count * (k + 1)].astype(
                target.dtype
            )


def add_kernel(ids, mine, *refs):
    come, (keep, give) = refs[:-2], refs[-2:]
    c = ids[0]
    half = keep.shape[0] // 2
    for h in range(2):
        for out, place in ((keep, c), (give, 1 - c)):
            here = pl.ds(pl.multiple_of((2 * h + place) * half, half), half)
            total = mine[here]
            for ref in come:
                total = total + ref[here].astype(f32)
            out[h * half : (h + 1) * half] = total.astype(out.dtype)


def final_kernel(scale, total_rows, ids, ours, theirs, totals, rstd, norm, mine, other, *outs):
    grad_a, grad_b, loss = outs
    c = ids[0]
    count, width = mine.shape
    lanes = width // 128
    back = [jnp.where(c == v, ours[...], theirs[...]) for v in range(2)]
    loss[...] = back[0][2 * lanes : 2 * lanes + 1] + back[1][2 * lanes : 2 * lanes + 1]
    _, diag_grad = diagonal(totals[...], total_rows)
    diag_grad = diag_grad * (1.0 / total_rows)
    for k in range(lanes):
        here = slice(k * 128, (k + 1) * 128)
        weight = diag_grad[:, here]
        same, cross = mine[:, here], other[:, here].astype(f32)
        for v, out in enumerate((grad_a, grad_b)):
            mean_grad = back[v][k : k + 1] + weight * totals[1 - v : 2 - v, here]
            mean_cross = back[v][lanes + k : lanes + k + 1] + weight * totals[2:3, here]
            grad = jnp.where(c == v, same, cross) + weight * norm[1 - v, :, here].astype(f32)
            out[:, here] = (
                (scale * rstd[v : v + 1, here])
                * (
                    grad
                    - mean_grad * (1.0 / total_rows)
                    - norm[v, :, here].astype(f32) * (mean_cross * (1.0 / total_rows))
                )
            ).astype(bf16)


def shards(view_a, view_b):
    count, width = view_a.shape
    total_rows = count * lax.axis_size(ROWS)
    places = [lax.axis_index(name) for name in ("c", "yl", "x")]
    ids = jnp.stack(places).astype(jnp.int32)
    half = count // 2
    block = shape(2, half, width, dtype=bf16)
    hops = lax.axis_size("z") // 2
    peers = lax.axis_size("x")

    first = places[0] == 0
    keep, give = jnp.where(first, view_a, view_b), jnp.where(first, view_b, view_a)
    near, rest, whole = call(
        split_kernel,
        "split",
        ids,
        [keep, swap(give, "c", 1)],
        [block, block, shape(4, half, width, dtype=bf16)],
    )

    far = swap(rest, RING, 1)
    whole_far, near_far, whole_near = swap(whole, RING, 3), swap(near, RING, 1), swap(whole, RING, 2)
    moments = add_moments(ids, [], [near], [far])
    opposite = shift(moments, hops)
    first = [shift(near, 1), shift(far, 1), shift(near, -1), shift(far, -1)]
    right, left = call(merge_kernel, "merge", ids, first, [shape(4, half, width, dtype=bf16)] * 2)
    right, left = tie((right, left), whole_far)
    moments = add_moments(ids, [moments], first[0::2], first[1::2])
    early, late = [right, left], []
    for hop in range(2, hops):
        if hop == 3:
            right, left = tie((right, left), whole_near, opposite, moments)
        right, left = shift(right, 1), shift(left, -1)
        last = hop == hops - 1
        early, late = early + [right] + [left] * (not last), late + [left] * last
        moments = add_moments(ids, [moments] + [opposite] * last, [right, left], [])
    right, left = tie((right, left), near_far)
    late += [shift(right[:2], 1), shift(left[2:], -1)]
    row_blocks = [near, rest, whole_near, far, near_far, whole_far]
    panel = 2 * half * lax.axis_size("z")
    piece = panel // peers
    pieces, cols, rows, stats = call(
        lambda *refs: gram_kernel(total_rows, *refs),
        "gram",
        ids,
        [moments] + [swap(moments, RING, k) for k in (1, 2, 3)] + row_blocks + early,
        [
            shape(peers - 1, piece, 4 * count, dtype=bf16),
            shape(panel, 2 * width, dtype=bf16),
            shape(4 * count, 2 * width, dtype=bf16),
            shape(4, width),
        ],
        flops=4 * count * panel * width * 3,
    )
    *parts, cols = call(
        last_gram_kernel,
        "last_gram",
        ids,
        [stats, rows, pieces, cols] + late,
        [shape(piece, 4 * count, dtype=bf16)] * peers + [shape(panel, 2 * width, dtype=bf16)],
        [pltpu.VMEM((peers, piece, 4 * count), bf16)],
        {4: peers},
    )

    come = [swap(parts[k], ("c", "x"), peers | k) for k in range(peers)]
    norm, rstd, sums = call(
        native_kernel,
        "native",
        ids,
        [view_a, view_b, stats[:2], swap(stats[:2], "c", 1)],
        [shape(2, count, width, dtype=bf16), shape(2, width), shape(4, width)],
    )
    sums = exchange_sum(sums, "c", (1,))
    sums = exchange_sum(sums, "yh", (1,))
    sums = exchange_sum(sums, "z", (1,))
    come[0] = tie(come[0], sums)
    low_gram, gram = call(
        reduce_kernel,
        "reduce",
        ids,
        come,
        [shape(4 * count, piece, dtype=bf16), shape(4 * count, piece)],
    )
    full = [low_gram] + [swap(low_gram, "x", k) for k in range(1, peers)]
    totals = exchange_sum(sums, "z", (2, 4))
    gram_other = swap(low_gram, "c", 1)
    full[1] = tie(full[1], totals, gram_other)
    lanes = width // 128


    def product(side, dtype, flops):
        return call(
            lambda *refs: product_kernel(
                2.0 * redund_weight / (total_rows * total_rows), side, peers, *refs
            ),
            "products",
            ids,
            full + [cols, rows],
            [shape(2 * count, width, dtype=dtype), shape(2 * count, width, dtype=bf16)]
            + [shape(2 * lanes, 128)],
            flops=flops,
        )

    leave_far, leave_both, far_sums = product(1, bf16, 8 * count * panel * width)
    mine, leave_near, near_sums = product(0, f32, 10**11)
    come_far, come_both = swap(leave_far, RING, 1), swap(leave_both, RING, 3)
    come_near = swap(leave_near, RING, 2)
    loss = call(
        lambda *refs: loss_kernel(total_rows, 1.0 / lax.axis_size(ROWS), *refs),
        "loss",
        ids,
        [gram, gram_other, tie(totals, far_sums)],
        [shape(8, 128)],
        flops=10**11,
    )[0]
    loss = loss + swap(loss, "x", 1) + swap(loss, "x", 2) + swap(loss, "x", 3)
    sums = exchange_sum(jnp.concatenate([near_sums, far_sums, loss]), "z", (1, 2, 4))
    sums = tie(sums, come_far, come_both, come_near)
    near_sums, far_sums = jnp.concatenate([sums[: 2 * lanes], sums[4 * lanes :]]), sums[2 * lanes :]
    back = near_sums + swap(near_sums, RING, 2) + swap(far_sums, RING, 1) + swap(far_sums, RING, 3)
    keep, give = call(
        add_kernel,
        "add",
        ids,
        [mine, come_far, come_both, come_near],
        [shape(count, width), shape(count, width, dtype=bf16)],
    )
    grad_a, grad_b, loss = call(
        lambda *refs: final_kernel(
            total_rows * total_rows / (redund_weight * WIDTH), total_rows, *refs
        ),
        "finish",
        ids,
        [back, swap(back, "c", 1), totals, rstd, norm, keep, swap(give, "c", 1)],
        [shape(count, width, dtype=bf16)] * 2 + [shape(1, 128)],
    )
    return grad_a, grad_b, loss[0, 0]


def solution(mesh):
    fine = Mesh(mesh.devices.reshape(8, 2, 2, 2, 4), ROWS + FEAT)
    return jax.shard_map(
        shards,
        mesh=fine,
        in_specs=(P(ROWS, FEAT), P(ROWS, FEAT)),
        out_specs=(P(ROWS, FEAT), P(ROWS, FEAT), P()),
        check_vma=False,
    )
```
